32 devices in a mesh: shard: 8 (over z, y), rep: 4 (over x, core).
Axes of the slice: x: 2, y: 2, z: 4, core: 2. Of those that a mesh axis runs over, the one named last changes fastest.
Arguments:
- embeddings: bfloat16 [8192, 512], P('shard'), may hold values from -6 to 6
- members: int32 [8, 1024], P('shard'), may hold values from -1 to 8191, as said below
Outputs:
- best: float32 [8, 1024], P('shard', 'rep')
The draws below stay inside these ranges and needn't reach their ends.
Inputs may be any that keep to these rules, and one draw needn't show every extreme that they name: In each cluster the valid row numbers come first, followed by -1 entries, and there are at least 128 valid ones. No row number appears twice anywhere. Among one cluster's members at most 128 lie in one aligned block of 1024 rows, and in every cluster some block holds exactly 128. Two clusters have all 1024 entries valid; the others have between a third and a half of 1024.
All inputs are finite; a program needn't handle non-finite values.
Results may differ from the reference program's by a relative error of at most 0.0014.
Values may be sent and summed in bfloat16 or wider, within the bound.
No kernel may reach another device: no remote copies, remote signals or barrier semaphores. Data moves between devices by JAX's collectives and lax.ppermute only.
A program may use at most 64 MiB of HBM per device.

```python
import jax
import jax.numpy as jnp
from jax import lax

D = 512
CAP = 1024
CLUSTERS = 8
ROWS_DEV = 1024
ROWS = 8192
SEND_CAP = 128


def draw_members(key, part):
    key_count, key_giant, key_source, key_slots, key_rows = jax.random.split(key, 5)
    lower_count = max(CAP // 3, SEND_CAP)
    small_count = jax.random.randint(key_count, (CLUSTERS,), lower_count, CAP // 2 + 1)
    order_giant = jax.random.permutation(key_giant, CLUSTERS)
    counts = jnp.where(order_giant < 2, CAP, small_count)
    first_source = jax.random.randint(key_source, (CLUSTERS,), 0, CLUSTERS)
    slot_keys = jax.random.split(key_slots, CLUSTERS)
    slot_order = jax.vmap(lambda subkey: jax.random.permutation(subkey, CAP))(slot_keys)
    source = slot_order // SEND_CAP
    later_flag = (source != first_source[:, None]).astype(jnp.int32)
    rank_order = jnp.argsort(later_flag, axis=1, stable=True)
    slot_order = jnp.take_along_axis(slot_order, rank_order, axis=1)
    source = slot_order // SEND_CAP
    bucket = slot_order % SEND_CAP
    row_keys = jax.random.split(key_rows, CLUSTERS)
    row_perm = jax.vmap(lambda subkey: jax.random.permutation(subkey, ROWS_DEV))(row_keys)
    cluster = jnp.arange(CLUSTERS, dtype=jnp.int32)[:, None]
    local_row = row_perm[source, cluster * SEND_CAP + bucket]
    row_ids = source * ROWS_DEV + local_row
    slot_index = jnp.arange(CAP, dtype=jnp.int32)[None, :]
    return jnp.where(slot_index < counts[:, None], row_ids, -1).astype(jnp.int32)


def shard_levels(key, extent, pieces, least, top_value):
    loudness, own = 1.0, jax.random.fold_in(key, 6)
    for dim, shards_of in pieces:
        heights = jnp.exp(jax.random.uniform(jax.random.fold_in(own, dim), (shards_of,), jnp.float32, least / len(pieces), top_value / len(pieces)))
        loudness = loudness * jnp.repeat(heights, extent[dim] // shards_of).reshape([-1 if axis == dim else 1 for axis in range(len(extent))])
    return loudness


def scatter_about(rng, shape, scale, most, cuts=(), kind=jnp.bfloat16):
    values = scale * jax.random.normal(rng, shape, jnp.float32)
    if cuts:
        values = values * shard_levels(rng, shape, cuts, -0.22, 0.18)
    return jnp.clip(values, -most, most).astype(kind)


def setup_inputs(seed: int = 0) -> dict:
    streams_of = jax.random.split(jax.random.key(seed), 3)
    return {
        "embeddings": scatter_about(streams_of[0], (ROWS, D), 1.0, 6.0, ((0, 8),)),
        "members": draw_members(jax.random.fold_in(streams_of[2], 71), 0),
    }


def unit_rows(embeddings):
    values = embeddings.astype(jnp.float32)
    total = lax.optimization_barrier(jnp.sum(values * values, axis=1, keepdims=True))
    return (values * lax.rsqrt(total + 1e-06)).astype(jnp.bfloat16)

def running_best(queries, positions, gathered, block_count, key_block):

    def update(block_index, current):
        start = (block_index * key_block).astype(jnp.int32)
        keys = lax.dynamic_slice_in_dim(gathered, start, key_block, 0)
        scores = lax.dot_general(queries, keys, (((1,), (1,)), ((), ())), preferred_element_type=jnp.float32)
        key_index = start + jnp.arange(key_block, dtype=jnp.int32)
        masked = jnp.where(key_index[None, :] < positions[:, None], scores, jnp.full_like(scores, -2.0))
        return jnp.maximum(current, lax.optimization_barrier(jnp.max(masked, axis=1)))
    initial = jnp.full((queries.shape[0],), -1.0, jnp.float32)
    return lax.fori_loop(jnp.int32(0), block_count.astype(jnp.int32), update, initial)

def reference(embeddings, members):
    unit = unit_rows(embeddings)
    block = min(512, CAP)

    def one_cluster(row_ids):
        valid = row_ids >= 0
        count = jnp.sum(valid.astype(jnp.int32))
        picked = jnp.take(unit, jnp.maximum(row_ids, 0).astype(jnp.int32), axis=0)
        gathered = jnp.where(valid[:, None], picked, jnp.zeros_like(picked)).astype(jnp.float32)

        def per_block(query_block, result):
            start = (query_block * block).astype(jnp.int32)
            queries = lax.dynamic_slice_in_dim(gathered, start, block, 0)
            positions = start + jnp.arange(block, dtype=jnp.int32)
            values = running_best(queries, positions, gathered, query_block + 1, block)
            values = jnp.where(positions < count, values, jnp.zeros_like(values))
            return lax.dynamic_update_slice_in_dim(result, values, start, 0)
        query_blocks = (count + block - 1) // block
        return lax.fori_loop(jnp.int32(0), query_blocks.astype(jnp.int32), per_block, jnp.zeros((CAP,), jnp.float32))
    return lax.map(one_cluster, members)
```

```python
import functools

import jax
import jax.numpy as jnp
from jax import lax
from jax.experimental import pallas as pl
from jax.experimental.pallas import tpu as pltpu
from jax.sharding import PartitionSpec as P

LANES = 128
FAR = 1e6


def nt_dot(a, b):
    return lax.dot_general(a, b, (((1,), (1,)), ((), ())), preferred_element_type=jnp.float32)


def dot(a, b):
    return jnp.dot(a, b, preferred_element_type=jnp.float32)


def ones_where(mask):
    return jnp.where(mask, 1.0, 0.0).astype(jnp.bfloat16)


def low_onehot(ids):
    return ones_where(lax.broadcasted_iota(jnp.int32, (LANES, ids.shape[1]), 0) == (ids & (LANES - 1)))


def high_onehot(ids, first_row, groups):
    high = (ids - first_row) >> 7
    return lax.broadcasted_iota(jnp.int32, (groups, ids.shape[1]), 0) == high


def slots_of(hit, groups):
    total = hit.shape[0]
    marks = hit.astype(jnp.bfloat16)
    before = ones_where(
        lax.broadcasted_iota(jnp.int32, (LANES, LANES), 0) < lax.broadcasted_iota(jnp.int32, (LANES, LANES), 1)
    )
    within = dot(marks, before)
    sums = dot(marks, jnp.ones((LANES, LANES), jnp.bfloat16)).astype(jnp.bfloat16)
    row = lax.broadcasted_iota(jnp.int32, (total, total), 0)
    col = lax.broadcasted_iota(jnp.int32, (total, total), 1)
    earlier = ones_where((col < row) & (col // groups == row // groups))
    return jnp.where(hit > 0.0, within + dot(earlier, sums), -1.0)


def selector(slots, send_cap):
    number = lax.broadcasted_iota(jnp.int32, (send_cap, LANES), 0).astype(jnp.float32)
    return jnp.concatenate([ones_where(slots[h : h + 1, :] == number) for h in range(slots.shape[0])], axis=1)


def block_id(distances):
    rep = lax.axis_index("rep")
    distance = jnp.int32(0)
    for r, d in enumerate(distances):
        distance = jnp.where(rep == r, jnp.int32(d), distance)
    return lax.axis_index("shard") ^ distance


def prepare_kernel(chunks, send_cap, ids_ref, rows_ref, unit_ref, own_ref, place_ref):
    rows_dev = rows_ref.shape[0]
    groups = rows_dev // LANES
    values = rows_ref[...].astype(jnp.float32)
    total = jnp.sum(values * values, axis=1, keepdims=True)
    unit_ref[...] = (values * lax.rsqrt(total + 1e-06)).astype(jnp.bfloat16)

    ids = ids_ref[...]
    low = low_onehot(ids)
    highs = [high_onehot(ids, block_id(d) * rows_dev, groups) for d in chunks]
    high = jnp.concatenate([jnp.where(h, 1.0, 0.0) for h in highs], axis=0)
    member = lax.broadcasted_iota(jnp.int32, (1, ids.shape[1]), 1)
    digits = (member >> 5).astype(jnp.float32), (member & 31).astype(jnp.float32)
    marks = jnp.concatenate([high, high * digits[0], high * digits[1]], axis=0).astype(jnp.bfloat16)
    found = nt_dot(marks, low)
    count = high.shape[0]
    hit = found[:count]
    position = found[count : 2 * count] * 32.0 + found[2 * count :]
    slots = slots_of(hit, groups)
    number = lax.broadcasted_iota(jnp.int32, (send_cap, LANES), 0).astype(jnp.float32)
    diagonal = lax.broadcasted_iota(jnp.int32, (send_cap, send_cap), 0) == lax.broadcasted_iota(
        jnp.int32, (send_cap, send_cap), 1
    )
    for c in range(len(chunks)):
        spread = jnp.zeros((send_cap, LANES), jnp.float32)
        for h in range(groups):
            g = c * groups + h
            spread += jnp.where(slots[g : g + 1, :] == number, position[g : g + 1, :] + 1.0, 0.0)
        column = jnp.sum(spread, axis=1, keepdims=True)
        line = jnp.sum(jnp.where(diagonal, column, 0.0), axis=0, keepdims=True)
        place_ref[c : c + 1, :] = jnp.where(line > 0.0, line - 1.0, FAR)
    own_ref[...] = dot(selector(slots[:groups], send_cap), unit_ref[...]).astype(jnp.bfloat16)


def select_kernel(count, send_cap, *refs):
    ids_refs, unit_ref, out_refs = refs[:count], refs[count], refs[count + 1 :]
    rows_dev = unit_ref.shape[0]
    groups = rows_dev // LANES
    first = lax.axis_index("shard") * rows_dev
    hits = []
    for ref in ids_refs:
        ids = ref[...]
        hits.append(nt_dot(ones_where(high_onehot(ids, first, 16)), low_onehot(ids))[:groups])
    slots = slots_of(jnp.concatenate(hits, axis=0), groups)
    unit = unit_ref[...]
    for t, ref in enumerate(out_refs):
        ref[...] = dot(selector(slots[t * groups : (t + 1) * groups], send_cap), unit).astype(jnp.bfloat16)


def best_kernel(stripe, *refs):
    place_ref, chunk_refs, out_ref, table_ref = refs[0], refs[1:-2], refs[-2], refs[-1]
    send_cap = chunk_refs[0].shape[0]
    for c, ref in enumerate(chunk_refs):
        table_ref[c * send_cap : (c + 1) * send_cap, :] = ref[...]
    place = place_ref[...]
    places = jnp.concatenate([place[c : c + 1, :] for c in range(len(chunk_refs))], axis=1)
    first = lax.axis_index("rep") * stripe
    query = (lax.broadcasted_iota(jnp.int32, (stripe, 1), 0) + first).astype(jnp.float32)
    table = table_ref[...]
    queries = dot(ones_where(places == query), table).astype(jnp.bfloat16)
    scores = nt_dot(queries, table)
    best = jnp.max(jnp.where(places < query, scores, -2.0), axis=1, keepdims=True)
    count = jnp.sum(jnp.where(places < FAR, 1.0, 0.0), axis=1, keepdims=True)
    best = jnp.where(query < count, jnp.maximum(best, -1.0), 0.0)
    diagonal = lax.broadcasted_iota(jnp.int32, (LANES, LANES), 0) == lax.broadcasted_iota(
        jnp.int32, (LANES, LANES), 1
    )
    for b in range(stripe // LANES):
        part = best[b * LANES : (b + 1) * LANES, :]
        out_ref[:, b * LANES : (b + 1) * LANES] = jnp.sum(jnp.where(diagonal, part, 0.0), axis=0, keepdims=True)


def vmem(count):
    return [pl.BlockSpec(memory_space=pltpu.VMEM)] * count


PARAMS = dict(compiler_params=pltpu.CompilerParams(vmem_limit_bytes=32 * 1024 * 1024))


def permute(array, distances):
    shards, helpers = lax.axis_size("shard"), lax.axis_size("rep")
    pairs = [
        (s * helpers + r, (s ^ distances[r]) * helpers + r) for s in range(shards) for r in range(helpers)
    ]
    return lax.ppermute(array, ("shard", "rep"), pairs)


def swap(array, mask):
    return lax.ppermute(array, "rep", [(r, r ^ mask) for r in range(lax.axis_size("rep"))])


def per_device(embeddings, members):
    shards = lax.axis_size("shard")
    helpers = lax.axis_size("rep")
    rows_dev, width = embeddings.shape
    capacity = members.shape[1]
    send_cap = capacity // shards
    stripe = capacity // helpers

    rounds = [[d + (r & 1) for r in range(helpers)] for d in range(shards - 2, 0, -2)] + [[1] * helpers]
    chunk_dist = [[0] * helpers] + rounds + [[d[r ^ 1] for r in range(helpers)] for d in rounds[:-1]]

    wanted = [permute(members, d) for d in rounds]
    rows = jax.ShapeDtypeStruct((send_cap, width), jnp.bfloat16)
    unit, own, place = pl.pallas_call(
        functools.partial(prepare_kernel, chunk_dist, send_cap),
        out_shape=(
            jax.ShapeDtypeStruct((rows_dev, width), jnp.bfloat16),
            rows,
            jax.ShapeDtypeStruct((len(chunk_dist), send_cap), jnp.float32),
        ),
        in_specs=vmem(2),
        out_specs=tuple(vmem(3)),
        cost_estimate=pl.CostEstimate(flops=10**9, bytes_accessed=3 * 2**20, transcendentals=0),
        **PARAMS,
    )(members, embeddings)
    sent = pl.pallas_call(
        functools.partial(select_kernel, len(rounds), send_cap),
        out_shape=(rows,) * len(rounds),
        in_specs=vmem(len(rounds) + 1),
        out_specs=tuple(vmem(len(rounds))),
        cost_estimate=pl.CostEstimate(flops=10**9, bytes_accessed=2 * 2**20, transcendentals=0),
        **PARAMS,
    )(*wanted, unit)
    fetched = [permute(rows, d) for rows, d in zip(sent, rounds)]
    shared = [swap(rows, 1) for rows in fetched[:-1]]
    chunks = [own] + fetched + shared
    return pl.pallas_call(
        functools.partial(best_kernel, stripe),
        out_shape=jax.ShapeDtypeStruct((1, stripe), jnp.float32),
        in_specs=vmem(len(chunks) + 1),
        out_specs=vmem(1)[0],
        scratch_shapes=[pltpu.VMEM((capacity, width), jnp.bfloat16)],
        cost_estimate=pl.CostEstimate(flops=10**9, bytes_accessed=2 * 2**20, transcendentals=0),
        **PARAMS,
    )(place, *chunks)


def unit_rows(embeddings):
    values = embeddings.astype(jnp.float32)
    total = jnp.sum(values * values, axis=1, keepdims=True)
    return (values * lax.rsqrt(total + 1e-06)).astype(jnp.bfloat16)


def fetch_rows(unit, wanted):
    picked = jnp.take(unit, jnp.maximum(wanted, 0), axis=0)
    return jnp.where((wanted >= 0)[..., None], picked, jnp.zeros_like(picked))


def running_best(queries, positions, gathered, block_count, key_block):

    def update(block_index, current):
        start = block_index * key_block
        keys = lax.dynamic_slice_in_dim(gathered, start, key_block, 0)
        scores = lax.dot_general(
            queries, keys, (((1,), (1,)), ((), ())), preferred_element_type=jnp.float32
        )
        key_index = start + jnp.arange(key_block, dtype=jnp.int32)
        masked = jnp.where(
            key_index[None, :] < positions[:, None], scores, jnp.full_like(scores, -2.0)
        )
        return jnp.maximum(current, jnp.max(masked, axis=1))

    initial = jnp.full((queries.shape[0],), -1.0, jnp.float32)
    return lax.fori_loop(jnp.int32(0), block_count, update, initial)


def per_device_many(embeddings, members):
    shards = lax.axis_size("shard")
    helpers = lax.axis_size("rep")
    helper_index = lax.axis_index("rep")
    rows_dev = embeddings.shape[0]
    width = embeddings.shape[1]
    capacity = members.shape[1]
    send_cap = capacity // shards
    unit = unit_rows(embeddings)
    row_ids = members[0]
    valid = row_ids >= 0
    count = jnp.sum(valid.astype(jnp.int32))
    source = jnp.where(valid, row_ids // rows_dev, -1)
    local_row = jnp.where(valid, row_ids - source * rows_dev, -1)
    onehot = (source[:, None] == jnp.arange(shards, dtype=jnp.int32)[None, :]).astype(jnp.int32)
    earlier = jnp.cumsum(onehot, axis=0) - onehot
    position = jnp.sum(earlier * onehot, axis=1)
    table_size = shards * send_cap
    flat_index = jnp.where(valid, source * send_cap + position, table_size)
    requests = jnp.full((table_size + 1,), -1, jnp.int32).at[flat_index].set(local_row)
    requests = requests[:table_size].reshape(shards, send_cap)
    wanted = lax.all_to_all(requests, "shard", split_axis=0, concat_axis=0, tiled=True)
    returned = lax.all_to_all(
        fetch_rows(unit, wanted), "shard", split_axis=0, concat_axis=0, tiled=True
    )
    table = returned.reshape(table_size, width)
    picked = jnp.take(table, jnp.minimum(flat_index, table_size - 1), axis=0)
    gathered = jnp.where(valid[:, None], picked, jnp.zeros_like(picked))
    stripe = capacity // helpers
    queries_all = lax.dynamic_slice_in_dim(gathered, helper_index * stripe, stripe, 0)
    positions_all = helper_index * stripe + jnp.arange(stripe, dtype=jnp.int32)
    key_block = min(512, capacity)
    needed = jnp.minimum(count, positions_all[-1])
    block_count = (needed + key_block - 1) // key_block
    values = running_best(queries_all, positions_all, gathered, block_count, key_block)
    pieces = jnp.where(positions_all < count, values, jnp.zeros_like(values))
    return pieces[None, :]


def solution(mesh):
    in_specs = (P("shard", None), P("shard", None))
    out_specs = P("shard", "rep")
    few = mesh.shape["shard"] == 8 and mesh.shape["rep"] == 4
    return jax.shard_map(
        per_device if few else per_device_many,
        mesh=mesh,
        in_specs=in_specs,
        out_specs=out_specs,
        check_vma=False,
    )
```

```python
import functools

import jax
import jax.numpy as jnp
from jax import lax
from jax.experimental import pallas as pl
from jax.experimental.pallas import tpu as pltpu
from jax.sharding import PartitionSpec as P

LANES = 128
FAR = 1e6


def nt_dot(a, b):
    return lax.dot_general(a, b, (((1,), (1,)), ((), ())), preferred_element_type=jnp.float32)


def dot(a, b):
    return jnp.dot(a, b, preferred_element_type=jnp.float32)


def ones_where(mask):
    return jnp.where(mask, 1.0, 0.0).astype(jnp.bfloat16)


def low_onehot(ids):
    return ones_where(lax.broadcasted_iota(jnp.int32, (LANES, ids.shape[1]), 0) == (ids & (LANES - 1)))


def high_onehot(ids, first_row, groups):
    high = (ids - first_row) >> 7
    return lax.broadcasted_iota(jnp.int32, (groups, ids.shape[1]), 0) == high


def slots_of(hit, groups):
    total = hit.shape[0]
    marks = hit.astype(jnp.bfloat16)
    before = ones_where(
        lax.broadcasted_iota(jnp.int32, (LANES, LANES), 0) < lax.broadcasted_iota(jnp.int32, (LANES, LANES), 1)
    )
    within = dot(marks, before)
    sums = dot(marks, jnp.ones((LANES, LANES), jnp.bfloat16)).astype(jnp.bfloat16)
    row = lax.broadcasted_iota(jnp.int32, (total, total), 0)
    col = lax.broadcasted_iota(jnp.int32, (total, total), 1)
    earlier = ones_where((col < row) & (col // groups == row // groups))
    return jnp.where(hit > 0.0, within + dot(earlier, sums), -1.0)


def selector(slots, numbers):
    return jnp.concatenate([ones_where(slots[h : h + 1, :] == numbers) for h in range(slots.shape[0])], axis=1)


def numbers_from(first, wanted, around):
    return ((lax.broadcasted_iota(jnp.int32, (wanted, LANES), 0) + first) & (around - 1)).astype(jnp.float32)


def by_rep(values):
    rep = lax.axis_index("rep")
    chosen = jnp.int32(values[0])
    for r, value in enumerate(values[1:], 1):
        chosen = jnp.where(rep == r, jnp.int32(value), chosen)
    return chosen


def unit_kernel(rows_ref, unit_ref):
    values = rows_ref[...].astype(jnp.float32)
    total = jnp.sum(values * values, axis=1, keepdims=True)
    unit_ref[...] = (values * lax.rsqrt(total + 1e-06)).astype(jnp.bfloat16)


def pick_rows(slots, numbers, unit):
    return dot(selector(slots, numbers), unit).astype(jnp.bfloat16)


def place_kernel(chunks, send_cap, ids_ref, rows_ref, own_ref, place_ref):
    rows_dev = rows_ref.shape[0]
    groups = rows_dev // LANES
    ids = ids_ref[...]
    low = low_onehot(ids)
    shard = lax.axis_index("shard")
    highs = [high_onehot(ids, (shard ^ by_rep(d)) * rows_dev, groups) for d, _ in chunks]
    high = jnp.concatenate([jnp.where(h, 1.0, 0.0) for h in highs], axis=0)
    member = lax.broadcasted_iota(jnp.int32, (1, ids.shape[1]), 1)
    digits = (member >> 5).astype(jnp.float32), (member & 31).astype(jnp.float32)
    marks = jnp.concatenate([high, high * digits[0], high * digits[1]], axis=0).astype(jnp.bfloat16)
    found = nt_dot(marks, low)
    count = high.shape[0]
    hit = found[:count]
    position = found[count : 2 * count] * 32.0 + found[2 * count :]
    slots = slots_of(hit, groups)
    diagonal = lax.broadcasted_iota(jnp.int32, (send_cap, send_cap), 0) == lax.broadcasted_iota(
        jnp.int32, (send_cap, send_cap), 1
    )
    for c, (_, first) in enumerate(chunks):
        numbers = numbers_from(by_rep(first), send_cap, send_cap)
        spread = jnp.zeros((send_cap, LANES), jnp.float32)
        for h in range(groups):
            g = c * groups + h
            spread += jnp.where(slots[g : g + 1, :] == numbers, position[g : g + 1, :] + 1.0, 0.0)
        column = jnp.sum(spread, axis=1, keepdims=True)
        line = jnp.sum(jnp.where(diagonal, column, 0.0), axis=0, keepdims=True)
        place_ref[c : c + 1, :] = jnp.where(line > 0.0, line - 1.0, FAR)
    numbers = numbers_from(0, send_cap, send_cap)
    own_ref[...] = pick_rows(slots[:groups], numbers, rows_ref[...])


def select_kernel(rounds, send_cap, *refs):
    count = len(rounds)
    ids_refs, rows_ref, out_refs = refs[:count], refs[count], refs[count + 1 :]
    rows_dev = rows_ref.shape[0]
    groups = rows_dev // LANES
    first_row = lax.axis_index("shard") * rows_dev
    hits = []
    for ref in ids_refs:
        ids = ref[...]
        hits.append(nt_dot(ones_where(high_onehot(ids, first_row, 16)), low_onehot(ids))[:groups])
    slots = slots_of(jnp.concatenate(hits, axis=0), groups)
    rows = rows_ref[...]
    for t, ref in enumerate(out_refs):
        numbers = numbers_from(by_rep(rounds[t][1]), ref.shape[0], send_cap)
        ref[...] = pick_rows(slots[t * groups : (t + 1) * groups], numbers, rows)


def hand_on_kernel(rows_ref, place_ref, out_ref):
    del place_ref
    out_ref[...] = rows_ref[...]


def best_kernel(stripe, *refs):
    place_ref, chunk_refs, out_ref, table_ref = refs[0], refs[1:-2], refs[-2], refs[-1]
    start = 0
    for ref in chunk_refs:
        table_ref[start : start + ref.shape[0], :] = ref[...]
        start += ref.shape[0]
    place = place_ref[...]
    places = jnp.concatenate([place[c : c + 1, :] for c in range(place.shape[0])], axis=1)
    first = lax.axis_index("rep") * stripe
    query = (lax.broadcasted_iota(jnp.int32, (stripe, 1), 0) + first).astype(jnp.float32)
    table = table_ref[...]
    queries = dot(ones_where(places == query), table).astype(jnp.bfloat16)
    scores = nt_dot(queries, table)
    best = jnp.max(jnp.where(places < query, scores, -2.0), axis=1, keepdims=True)
    count = jnp.sum(jnp.where(places < FAR, 1.0, 0.0), axis=1, keepdims=True)
    best = jnp.where(query < count, jnp.maximum(best, -1.0), 0.0)
    diagonal = lax.broadcasted_iota(jnp.int32, (LANES, LANES), 0) == lax.broadcasted_iota(
        jnp.int32, (LANES, LANES), 1
    )
    for b in range(stripe // LANES):
        part = best[b * LANES : (b + 1) * LANES, :]
        out_ref[:, b * LANES : (b + 1) * LANES] = jnp.sum(jnp.where(diagonal, part, 0.0), axis=0, keepdims=True)


def vmem(count):
    return [pl.BlockSpec(memory_space=pltpu.VMEM)] * count


PARAMS = dict(compiler_params=pltpu.CompilerParams(vmem_limit_bytes=32 * 1024 * 1024))


def permute(array, distances):
    shards, helpers = lax.axis_size("shard"), lax.axis_size("rep")
    pairs = [
        (s * helpers + r, (s ^ distances[r]) * helpers + r) for s in range(shards) for r in range(helpers)
    ]
    return lax.ppermute(array, ("shard", "rep"), pairs)


def swap(array, mask):
    return lax.ppermute(array, "rep", [(r, r ^ mask) for r in range(lax.axis_size("rep"))])


def per_device(embeddings, members):
    shards = lax.axis_size("shard")
    helpers = lax.axis_size("rep")
    rows_dev, width = embeddings.shape
    capacity = members.shape[1]
    send_cap = capacity // shards
    stripe = capacity // helpers

    half = send_cap // 2
    reps = range(helpers)
    zero = [0] * helpers
    far = ([shards - 2 + (r >> 1) for r in reps], [half * (r & 1) for r in reps])
    pairs = [([d + (r & 1) for r in reps], zero) for d in range(shards - 4, 0, -2)]
    rounds = [far] + pairs + [([1] * helpers, zero)]
    chunks = [(zero, zero), rounds[-1]]
    chunks += pairs + [([d[r ^ 1] for r in reps], zero) for d, _ in pairs]
    chunks += [far, ([far[0][r ^ 2] for r in reps], far[1])]

    wanted = [permute(members, d) for d, _ in rounds]
    def rows(count):
        return jax.ShapeDtypeStruct((count, width), jnp.bfloat16)

    unit = pl.pallas_call(
        unit_kernel,
        out_shape=rows(rows_dev),
        in_specs=vmem(1),
        out_specs=vmem(1)[0],
        cost_estimate=pl.CostEstimate(flops=10**7, bytes_accessed=2 * 2**20, transcendentals=0),
        **PARAMS,
    )(embeddings)
    sent = [None] * len(rounds)
    for group in ([0, 1], list(range(2, len(rounds)))):
        picked = pl.pallas_call(
            functools.partial(select_kernel, [rounds[t] for t in group], send_cap),
            out_shape=tuple(rows(half if t == 0 else send_cap) for t in group),
            in_specs=vmem(len(group) + 1),
            out_specs=tuple(vmem(len(group))),
            cost_estimate=pl.CostEstimate(flops=10**9, bytes_accessed=2 * 2**20, transcendentals=0),
            **PARAMS,
        )(*[wanted[t] for t in group], unit)
        for t, part in zip(group, picked):
            sent[t] = part
    fetched = [permute(part, d) for part, (d, _) in zip(sent, rounds)]
    own, place = pl.pallas_call(
        functools.partial(place_kernel, chunks, send_cap),
        out_shape=(rows(send_cap), jax.ShapeDtypeStruct((len(chunks), send_cap), jnp.float32)),
        in_specs=vmem(2),
        out_specs=tuple(vmem(2)),
        cost_estimate=pl.CostEstimate(flops=10**9, bytes_accessed=2 * 2**20, transcendentals=0),
        **PARAMS,
    )(members, unit)
    handed = pl.pallas_call(
        hand_on_kernel,
        out_shape=rows(half),
        in_specs=vmem(2),
        out_specs=vmem(1)[0],
        cost_estimate=pl.CostEstimate(flops=10**9, bytes_accessed=2**17, transcendentals=0),
        **PARAMS,
    )(fetched[0], place)
    crossed = swap(handed, 2)
    parts = [own, fetched[-1]] + fetched[1:-1] + [swap(part, 1) for part in fetched[1:-1]]
    parts += [fetched[0], swap(fetched[0], 1), crossed, swap(crossed, 1)]
    return pl.pallas_call(
        functools.partial(best_kernel, stripe),
        out_shape=jax.ShapeDtypeStruct((1, stripe), jnp.float32),
        in_specs=vmem(len(parts) + 1),
        out_specs=vmem(1)[0],
        scratch_shapes=[pltpu.VMEM((capacity, width), jnp.bfloat16)],
        cost_estimate=pl.CostEstimate(flops=10**9, bytes_accessed=2 * 2**20, transcendentals=0),
        **PARAMS,
    )(place, *parts)


def unit_rows(embeddings):
    values = embeddings.astype(jnp.float32)
    total = jnp.sum(values * values, axis=1, keepdims=True)
    return (values * lax.rsqrt(total + 1e-06)).astype(jnp.bfloat16)


def fetch_rows(unit, wanted):
    picked = jnp.take(unit, jnp.maximum(wanted, 0), axis=0)
    return jnp.where((wanted >= 0)[..., None], picked, jnp.zeros_like(picked))


def running_best(queries, positions, gathered, block_count, key_block):

    def update(block_index, current):
        start = block_index * key_block
        keys = lax.dynamic_slice_in_dim(gathered, start, key_block, 0)
        scores = lax.dot_general(
            queries, keys, (((1,), (1,)), ((), ())), preferred_element_type=jnp.float32
        )
        key_index = start + jnp.arange(key_block, dtype=jnp.int32)
        masked = jnp.where(
            key_index[None, :] < positions[:, None], scores, jnp.full_like(scores, -2.0)
        )
        return jnp.maximum(current, jnp.max(masked, axis=1))

    initial = jnp.full((queries.shape[0],), -1.0, jnp.float32)
    return lax.fori_loop(jnp.int32(0), block_count, update, initial)


def per_device_many(embeddings, members):
    shards = lax.axis_size("shard")
    helpers = lax.axis_size("rep")
    helper_index = lax.axis_index("rep")
    rows_dev = embeddings.shape[0]
    width = embeddings.shape[1]
    capacity = members.shape[1]
    send_cap = capacity // shards
    unit = unit_rows(embeddings)
    row_ids = members[0]
    valid = row_ids >= 0
    count = jnp.sum(valid.astype(jnp.int32))
    source = jnp.where(valid, row_ids // rows_dev, -1)
    local_row = jnp.where(valid, row_ids - source * rows_dev, -1)
    onehot = (source[:, None] == jnp.arange(shards, dtype=jnp.int32)[None, :]).astype(jnp.int32)
    earlier = jnp.cumsum(onehot, axis=0) - onehot
    position = jnp.sum(earlier * onehot, axis=1)
    table_size = shards * send_cap
    flat_index = jnp.where(valid, source * send_cap + position, table_size)
    requests = jnp.full((table_size + 1,), -1, jnp.int32).at[flat_index].set(local_row)
    requests = requests[:table_size].reshape(shards, send_cap)
    wanted = lax.all_to_all(requests, "shard", split_axis=0, concat_axis=0, tiled=True)
    returned = lax.all_to_all(
        fetch_rows(unit, wanted), "shard", split_axis=0, concat_axis=0, tiled=True
    )
    table = returned.reshape(table_size, width)
    picked = jnp.take(table, jnp.minimum(flat_index, table_size - 1), axis=0)
    gathered = jnp.where(valid[:, None], picked, jnp.zeros_like(picked))
    stripe = capacity // helpers
    queries_all = lax.dynamic_slice_in_dim(gathered, helper_index * stripe, stripe, 0)
    positions_all = helper_index * stripe + jnp.arange(stripe, dtype=jnp.int32)
    key_block = min(512, capacity)
    needed = jnp.minimum(count, positions_all[-1])
    block_count = (needed + key_block - 1) // key_block
    values = running_best(queries_all, positions_all, gathered, block_count, key_block)
    pieces = jnp.where(positions_all < count, values, jnp.zeros_like(values))
    return pieces[None, :]


def solution(mesh):
    in_specs = (P("shard", None), P("shard", None))
    out_specs = P("shard", "rep")
    few = mesh.shape["shard"] == 8 and mesh.shape["rep"] == 4
    return jax.shard_map(
        per_device if few else per_device_many,
        mesh=mesh,
        in_specs=in_specs,
        out_specs=out_specs,
        check_vma=False,
    )
```

```python
import functools

import jax
import jax.numpy as jnp
from jax import lax
from jax.experimental import pallas as pl
from jax.experimental.pallas import tpu as pltpu
from jax.sharding import PartitionSpec as P

LANES = 128
FAR = 1e6


def nt_dot(a, b):
    return lax.dot_general(a, b, (((1,), (1,)), ((), ())), preferred_element_type=jnp.float32)


def dot(a, b):
    return jnp.dot(a, b, preferred_element_type=jnp.float32)


def ones_where(mask):
    return jnp.where(mask, 1.0, 0.0).astype(jnp.bfloat16)


def low_onehot(ids):
    return ones_where(lax.broadcasted_iota(jnp.int32, (LANES, ids.shape[1]), 0) == (ids & (LANES - 1)))


def high_onehot(ids, first_row, groups):
    high = (ids - first_row) >> 7
    return lax.broadcasted_iota(jnp.int32, (groups, ids.shape[1]), 0) == high


def slots_of(hit, groups):
    total = hit.shape[0]
    marks = hit.astype(jnp.bfloat16)
    before = ones_where(
        lax.broadcasted_iota(jnp.int32, (LANES, LANES), 0) < lax.broadcasted_iota(jnp.int32, (LANES, LANES), 1)
    )
    within = dot(marks, before)
    sums = dot(marks, jnp.ones((LANES, LANES), jnp.bfloat16)).astype(jnp.bfloat16)
    row = lax.broadcasted_iota(jnp.int32, (total, total), 0)
    col = lax.broadcasted_iota(jnp.int32, (total, total), 1)
    earlier = ones_where((col < row) & (col // groups == row // groups))
    return jnp.where(hit > 0.0, within + dot(earlier, sums), -1.0)


def selector(slots, numbers):
    return jnp.concatenate([ones_where(slots[h : h + 1, :] == numbers) for h in range(slots.shape[0])], axis=1)


def numbers_from(first, wanted, around):
    return ((lax.broadcasted_iota(jnp.int32, (wanted, LANES), 0) + first) & (around - 1)).astype(jnp.float32)


def by_rep(values):
    rep = lax.axis_index("rep")
    chosen = jnp.int32(values[0])
    for r, value in enumerate(values[1:], 1):
        chosen = jnp.where(rep == r, jnp.int32(value), chosen)
    return chosen


def zero_kernel(out_ref):
    out_ref[...] = jnp.zeros(out_ref.shape, out_ref.dtype)


def unit_kernel(rows_ref, tick_ref, unit_ref):
    del tick_ref
    values = rows_ref[...].astype(jnp.float32)
    total = jnp.sum(values * values, axis=1, keepdims=True)
    unit_ref[...] = (values * lax.rsqrt(total + 1e-06)).astype(jnp.bfloat16)


def pick_rows(slots, numbers, unit):
    return dot(selector(slots, numbers), unit).astype(jnp.bfloat16)


def place_kernel(chunks, send_cap, ids_ref, unit_ref, place_ref, own_ref):
    groups = unit_ref.shape[0] // LANES
    ids = ids_ref[...]
    low = low_onehot(ids)
    shard = lax.axis_index("shard")
    highs = [high_onehot(ids, (shard ^ by_rep(d)) * groups * LANES, groups) for d, _ in chunks]
    high = jnp.concatenate([jnp.where(h, 1.0, 0.0) for h in highs], axis=0)
    member = lax.broadcasted_iota(jnp.int32, (1, ids.shape[1]), 1)
    digits = (member >> 5).astype(jnp.float32), (member & 31).astype(jnp.float32)
    marks = jnp.concatenate([high, high * digits[0], high * digits[1]], axis=0).astype(jnp.bfloat16)
    found = nt_dot(marks, low)
    count = high.shape[0]
    hit = found[:count]
    position = found[count : 2 * count] * 32.0 + found[2 * count :]
    slots = slots_of(hit, groups)
    diagonal = lax.broadcasted_iota(jnp.int32, (send_cap, send_cap), 0) == lax.broadcasted_iota(
        jnp.int32, (send_cap, send_cap), 1
    )
    for c, (_, first) in enumerate(chunks):
        numbers = numbers_from(by_rep(first), send_cap, send_cap)
        spread = jnp.zeros((send_cap, LANES), jnp.float32)
        for h in range(groups):
            g = c * groups + h
            spread += jnp.where(slots[g : g + 1, :] == numbers, position[g : g + 1, :] + 1.0, 0.0)
        column = jnp.sum(spread, axis=1, keepdims=True)
        line = jnp.sum(jnp.where(diagonal, column, 0.0), axis=0, keepdims=True)
        place_ref[c : c + 1, :] = jnp.where(line > 0.0, line - 1.0, FAR)
    own_ref[...] = pick_rows(slots[:groups], numbers_from(0, send_cap, send_cap), unit_ref[...])


def select_kernel(rounds, send_cap, *refs):
    count = len(rounds)
    ids_refs, unit_ref, out_refs = refs[:count], refs[count], refs[-count:]
    rows_dev = unit_ref.shape[0]
    groups = rows_dev // LANES
    first_row = lax.axis_index("shard") * rows_dev
    hits = []
    for ref in ids_refs:
        ids = ref[...]
        hits.append(nt_dot(ones_where(high_onehot(ids, first_row, 16)), low_onehot(ids))[:groups])
    slots = slots_of(jnp.concatenate(hits, axis=0), groups)
    unit = unit_ref[...]
    for t in range(count):
        ref = out_refs[t]
        numbers = numbers_from(by_rep(rounds[t][1]), ref.shape[0], send_cap)
        ref[...] = pick_rows(slots[t * groups : (t + 1) * groups], numbers, unit)


def hand_on_kernel(rows_ref, *refs):
    refs[-1][:16, :] = rows_ref[:16, :]


def best_kernel(stripe, *refs):
    place_ref, chunk_refs, out_ref, table_ref = refs[0], refs[1:-2], refs[-2], refs[-1]
    start = 0
    for ref in chunk_refs:
        table_ref[start : start + ref.shape[0], :] = ref[...]
        start += ref.shape[0]
    place = place_ref[...]
    places = jnp.concatenate([place[c : c + 1, :] for c in range(place.shape[0])], axis=1)
    first = lax.axis_index("rep") * stripe
    query = (lax.broadcasted_iota(jnp.int32, (stripe, 1), 0) + first).astype(jnp.float32)
    table = table_ref[...]
    queries = dot(ones_where(places == query), table).astype(jnp.bfloat16)
    scores = nt_dot(queries, table)
    best = jnp.max(jnp.where(places < query, scores, -2.0), axis=1, keepdims=True)
    count = jnp.sum(jnp.where(places < FAR, 1.0, 0.0), axis=1, keepdims=True)
    best = jnp.where(query < count, jnp.maximum(best, -1.0), 0.0)
    diagonal = lax.broadcasted_iota(jnp.int32, (LANES, LANES), 0) == lax.broadcasted_iota(
        jnp.int32, (LANES, LANES), 1
    )
    for b in range(stripe // LANES):
        part = best[b * LANES : (b + 1) * LANES, :]
        out_ref[:, b * LANES : (b + 1) * LANES] = jnp.sum(jnp.where(diagonal, part, 0.0), axis=0, keepdims=True)


def vmem(count):
    return [pl.BlockSpec(memory_space=pltpu.VMEM)] * count


PARAMS = dict(compiler_params=pltpu.CompilerParams(vmem_limit_bytes=32 * 1024 * 1024))


def permute(array, distances):
    shards, helpers = lax.axis_size("shard"), lax.axis_size("rep")
    pairs = [
        (s * helpers + r, (s ^ distances[r]) * helpers + r) for s in range(shards) for r in range(helpers)
    ]
    return lax.ppermute(array, ("shard", "rep"), pairs)


def swap(array, mask):
    return lax.ppermute(array, "rep", [(r, r ^ mask) for r in range(lax.axis_size("rep"))])


def per_device(embeddings, members):
    shards = lax.axis_size("shard")
    helpers = lax.axis_size("rep")
    rows_dev, width = embeddings.shape
    capacity = members.shape[1]
    send_cap = capacity // shards
    stripe = capacity // helpers

    half = send_cap // 2
    reps = range(helpers)
    zero = [0] * helpers
    far = ([shards - 4 + (r >> 1) for r in reps], [half * (r & 1) for r in reps])
    pairs = [([d + (r & 1) for r in reps], zero) for d in (shards - 2, shards - 6)]
    rounds = [far] + pairs + [([1] * helpers, zero)]
    chunks = [(zero, zero), rounds[-1]]
    chunks += pairs + [([d[r ^ 1] for r in reps], zero) for d, _ in pairs]
    chunks += [far, ([far[0][r ^ 2] for r in reps], far[1])]

    wanted = [permute(members, d) for d, _ in rounds]
    def rows(count):
        return jax.ShapeDtypeStruct((count, width), jnp.bfloat16)

    tick = pl.pallas_call(
        zero_kernel,
        out_shape=jax.ShapeDtypeStruct((8, LANES), jnp.float32),
        out_specs=vmem(1)[0],
        cost_estimate=pl.CostEstimate(flops=5 * 10**8, bytes_accessed=2**12, transcendentals=0),
        **PARAMS,
    )()
    unit = pl.pallas_call(
        unit_kernel,
        out_shape=rows(rows_dev),
        in_specs=vmem(2),
        out_specs=vmem(1)[0],
        cost_estimate=pl.CostEstimate(flops=10**6, bytes_accessed=2**18, transcendentals=0),
        **PARAMS,
    )(embeddings, tick)
    place, own = pl.pallas_call(
        functools.partial(place_kernel, chunks, send_cap),
        out_shape=(jax.ShapeDtypeStruct((len(chunks), send_cap), jnp.float32), rows(send_cap)),
        in_specs=vmem(2),
        out_specs=tuple(vmem(2)),
        cost_estimate=pl.CostEstimate(flops=10**9, bytes_accessed=2**12, transcendentals=0),
        **PARAMS,
    )(members, unit)
    sent = []
    after = []
    for group in ([0], [1], [2, 3]):
        sent += pl.pallas_call(
            functools.partial(select_kernel, [rounds[t] for t in group], send_cap),
            out_shape=tuple(rows(half if t == 0 else send_cap) for t in group),
            in_specs=vmem(len(group) + 1 + len(after)),
            out_specs=tuple(vmem(len(group))),
            cost_estimate=pl.CostEstimate(flops=10**9, bytes_accessed=2**12, transcendentals=0),
            **PARAMS,
        )(*[wanted[t] for t in group], unit, *after)
        after = sent[-1:]
    fetched = [permute(part, d) for part, (d, _) in zip(sent, rounds)]

    def hand_on(part, flops, *others):
        return pl.pallas_call(
            hand_on_kernel,
            out_shape=rows(part.shape[0]),
            in_specs=vmem(1 + len(others)),
            out_specs=vmem(1)[0],
            input_output_aliases={0: 0},
            cost_estimate=pl.CostEstimate(flops=flops, bytes_accessed=2**12, transcendentals=0),
            **PARAMS,
        )(part, *others)

    fetched[0] = hand_on(fetched[0], 10**9)
    fetched[1] = hand_on(fetched[1], 8 * 10**8)
    fetched[2] = hand_on(fetched[2], 10**6, place)
    crossed = swap(fetched[0], 2)
    parts = [own, fetched[-1]] + fetched[1:-1] + [swap(part, 1) for part in fetched[1:-1]]
    parts += [fetched[0], swap(fetched[0], 1), crossed, swap(crossed, 1)]
    return pl.pallas_call(
        functools.partial(best_kernel, stripe),
        out_shape=jax.ShapeDtypeStruct((1, stripe), jnp.float32),
        in_specs=vmem(len(parts) + 1),
        out_specs=vmem(1)[0],
        scratch_shapes=[pltpu.VMEM((capacity, width), jnp.bfloat16)],
        cost_estimate=pl.CostEstimate(flops=10**9, bytes_accessed=2 * 2**20, transcendentals=0),
        **PARAMS,
    )(place, *parts)


def unit_rows(embeddings):
    values = embeddings.astype(jnp.float32)
    total = jnp.sum(values * values, axis=1, keepdims=True)
    return (values * lax.rsqrt(total + 1e-06)).astype(jnp.bfloat16)


def fetch_rows(unit, wanted):
    picked = jnp.take(unit, jnp.maximum(wanted, 0), axis=0)
    return jnp.where((wanted >= 0)[..., None], picked, jnp.zeros_like(picked))


def running_best(queries, positions, gathered, block_count, key_block):

    def update(block_index, current):
        start = block_index * key_block
        keys = lax.dynamic_slice_in_dim(gathered, start, key_block, 0)
        scores = lax.dot_general(
            queries, keys, (((1,), (1,)), ((), ())), preferred_element_type=jnp.float32
        )
        key_index = start + jnp.arange(key_block, dtype=jnp.int32)
        masked = jnp.where(
            key_index[None, :] < positions[:, None], scores, jnp.full_like(scores, -2.0)
        )
        return jnp.maximum(current, jnp.max(masked, axis=1))

    initial = jnp.full((queries.shape[0],), -1.0, jnp.float32)
    return lax.fori_loop(jnp.int32(0), block_count, update, initial)


def per_device_many(embeddings, members):
    shards = lax.axis_size("shard")
    helpers = lax.axis_size("rep")
    helper_index = lax.axis_index("rep")
    rows_dev = embeddings.shape[0]
    width = embeddings.shape[1]
    capacity = members.shape[1]
    send_cap = capacity // shards
    unit = unit_rows(embeddings)
    row_ids = members[0]
    valid = row_ids >= 0
    count = jnp.sum(valid.astype(jnp.int32))
    source = jnp.where(valid, row_ids // rows_dev, -1)
    local_row = jnp.where(valid, row_ids - source * rows_dev, -1)
    onehot = (source[:, None] == jnp.arange(shards, dtype=jnp.int32)[None, :]).astype(jnp.int32)
    earlier = jnp.cumsum(onehot, axis=0) - onehot
    position = jnp.sum(earlier * onehot, axis=1)
    table_size = shards * send_cap
    flat_index = jnp.where(valid, source * send_cap + position, table_size)
    requests = jnp.full((table_size + 1,), -1, jnp.int32).at[flat_index].set(local_row)
    requests = requests[:table_size].reshape(shards, send_cap)
    wanted = lax.all_to_all(requests, "shard", split_axis=0, concat_axis=0, tiled=True)
    returned = lax.all_to_all(
        fetch_rows(unit, wanted), "shard", split_axis=0, concat_axis=0, tiled=True
    )
    table = returned.reshape(table_size, width)
    picked = jnp.take(table, jnp.minimum(flat_index, table_size - 1), axis=0)
    gathered = jnp.where(valid[:, None], picked, jnp.zeros_like(picked))
    stripe = capacity // helpers
    queries_all = lax.dynamic_slice_in_dim(gathered, helper_index * stripe, stripe, 0)
    positions_all = helper_index * stripe + jnp.arange(stripe, dtype=jnp.int32)
    key_block = min(512, capacity)
    needed = jnp.minimum(count, positions_all[-1])
    block_count = (needed + key_block - 1) // key_block
    values = running_best(queries_all, positions_all, gathered, block_count, key_block)
    pieces = jnp.where(positions_all < count, values, jnp.zeros_like(values))
    return pieces[None, :]


def solution(mesh):
    in_specs = (P("shard", None), P("shard", None))
    out_specs = P("shard", "rep")
    few = mesh.shape["shard"] == 8 and mesh.shape["rep"] == 4
    return jax.shard_map(
        per_device if few else per_device_many,
        mesh=mesh,
        in_specs=in_specs,
        out_specs=out_specs,
        check_vma=False,
    )
```

```python
import functools

import jax
import jax.numpy as jnp
from jax import lax
from jax.experimental import pallas as pl
from jax.experimental.pallas import tpu as pltpu
from jax.sharding import PartitionSpec as P

LANES = 128
FAR = 1e6


def nt_dot(a, b):
    return lax.dot_general(a, b, (((1,), (1,)), ((), ())), preferred_element_type=jnp.float32)


def dot(a, b):
    return jnp.dot(a, b, preferred_element_type=jnp.float32)


def ones_where(mask):
    return jnp.where(mask, 1.0, 0.0).astype(jnp.bfloat16)


def low_onehot(ids):
    return ones_where(lax.broadcasted_iota(jnp.int32, (LANES, ids.shape[1]), 0) == (ids & (LANES - 1)))


def high_onehot(ids, first_row, groups):
    high = (ids - first_row) >> 7
    return lax.broadcasted_iota(jnp.int32, (groups, ids.shape[1]), 0) == high


def slots_of(hit, groups):
    total = hit.shape[0]
    marks = hit.astype(jnp.bfloat16)
    before = ones_where(
        lax.broadcasted_iota(jnp.int32, (LANES, LANES), 0) < lax.broadcasted_iota(jnp.int32, (LANES, LANES), 1)
    )
    within = dot(marks, before)
    sums = dot(marks, jnp.ones((LANES, LANES), jnp.bfloat16)).astype(jnp.bfloat16)
    row = lax.broadcasted_iota(jnp.int32, (total, total), 0)
    col = lax.broadcasted_iota(jnp.int32, (total, total), 1)
    earlier = ones_where((col < row) & (col // groups == row // groups))
    return jnp.where(hit > 0.0, within + dot(earlier, sums), -1.0)


def selector(slots, numbers):
    return jnp.concatenate([ones_where(slots[h : h + 1, :] == numbers) for h in range(slots.shape[0])], axis=1)


def numbers_from(first, wanted, around):
    return ((lax.broadcasted_iota(jnp.int32, (wanted, LANES), 0) + first) & (around - 1)).astype(jnp.float32)


def by_rep(values):
    rep = lax.axis_index("rep")
    chosen = jnp.int32(values[0])
    for r, value in enumerate(values[1:], 1):
        chosen = jnp.where(rep == r, jnp.int32(value), chosen)
    return chosen


def zero_kernel(out_ref):
    out_ref[...] = jnp.zeros(out_ref.shape, out_ref.dtype)


def pick_rows(slots, numbers, rows):
    values = dot(selector(slots, numbers), rows)
    total = jnp.sum(values * values, axis=1, keepdims=True)
    return (values * lax.rsqrt(total + 1e-06)).astype(jnp.bfloat16)


def place_kernel(chunks, send_cap, ids_ref, rows_ref, *refs):
    place_ref, own_ref = refs[-2:]
    groups = rows_ref.shape[0] // LANES
    ids = ids_ref[...]
    low = low_onehot(ids)
    shard = lax.axis_index("shard")
    highs = [high_onehot(ids, (shard ^ by_rep(d)) * groups * LANES, groups) for d, _ in chunks]
    high = jnp.concatenate([jnp.where(h, 1.0, 0.0) for h in highs], axis=0)
    member = lax.broadcasted_iota(jnp.int32, (1, ids.shape[1]), 1)
    digits = (member >> 5).astype(jnp.float32), (member & 31).astype(jnp.float32)
    marks = jnp.concatenate([high, high * digits[0], high * digits[1]], axis=0).astype(jnp.bfloat16)
    found = nt_dot(marks, low)
    count = high.shape[0]
    hit = found[:count]
    position = found[count : 2 * count] * 32.0 + found[2 * count :]
    slots = slots_of(hit, groups)
    diagonal = lax.broadcasted_iota(jnp.int32, (send_cap, send_cap), 0) == lax.broadcasted_iota(
        jnp.int32, (send_cap, send_cap), 1
    )
    for c, (_, first) in enumerate(chunks):
        numbers = numbers_from(by_rep(first), send_cap, send_cap)
        spread = jnp.zeros((send_cap, LANES), jnp.float32)
        for h in range(groups):
            g = c * groups + h
            spread += jnp.where(slots[g : g + 1, :] == numbers, position[g : g + 1, :] + 1.0, 0.0)
        column = jnp.sum(spread, axis=1, keepdims=True)
        line = jnp.sum(jnp.where(diagonal, column, 0.0), axis=0, keepdims=True)
        place_ref[c : c + 1, :] = jnp.where(line > 0.0, line - 1.0, FAR)
    own_ref[...] = pick_rows(slots[:groups], numbers_from(0, send_cap, send_cap), rows_ref[...])


def select_kernel(rounds, send_cap, *refs):
    count = len(rounds)
    ids_refs, rows_ref, out_refs = refs[:count], refs[count], refs[-count:]
    rows_dev = rows_ref.shape[0]
    groups = rows_dev // LANES
    first_row = lax.axis_index("shard") * rows_dev
    hits = []
    for ref in ids_refs:
        ids = ref[...]
        hits.append(nt_dot(ones_where(high_onehot(ids, first_row, 16)), low_onehot(ids))[:groups])
    slots = slots_of(jnp.concatenate(hits, axis=0), groups)
    rows = rows_ref[...]
    for t in range(count):
        ref = out_refs[t]
        numbers = numbers_from(by_rep(rounds[t][1]), ref.shape[0], send_cap)
        ref[...] = pick_rows(slots[t * groups : (t + 1) * groups], numbers, rows)


def hand_on_kernel(rows_ref, *refs):
    refs[-1][:16, :] = rows_ref[:16, :]


def best_kernel(stripe, *refs):
    place_ref, chunk_refs, out_ref, table_ref = refs[0], refs[1:-2], refs[-2], refs[-1]
    send_cap, start, near = place_ref.shape[1], 0, table_ref.shape[0] - place_ref.shape[1]
    for ref in chunk_refs:
        row = start if start < send_cap else start + send_cap if start < near else start - near + send_cap
        table_ref[row : row + ref.shape[0], :] = ref[...]
        start += ref.shape[0]
    place = place_ref[...]
    places = jnp.concatenate([place[c : c + 1, :] for c in range(place.shape[0])], axis=1)
    first = lax.axis_index("rep") * stripe
    query = (lax.broadcasted_iota(jnp.int32, (stripe, 1), 0) + first).astype(jnp.float32)
    table = table_ref[...]
    queries = dot(ones_where(places == query), table).astype(jnp.bfloat16)
    scores = nt_dot(queries, table)
    best = jnp.max(jnp.where(places < query, scores, -2.0), axis=1, keepdims=True)
    count = jnp.sum(jnp.where(places < FAR, 1.0, 0.0), axis=1, keepdims=True)
    best = jnp.where(query < count, jnp.maximum(best, -1.0), 0.0)
    diagonal = lax.broadcasted_iota(jnp.int32, (LANES, LANES), 0) == lax.broadcasted_iota(
        jnp.int32, (LANES, LANES), 1
    )
    for b in range(stripe // LANES):
        part = best[b * LANES : (b + 1) * LANES, :]
        out_ref[:, b * LANES : (b + 1) * LANES] = jnp.sum(jnp.where(diagonal, part, 0.0), axis=0, keepdims=True)


def vmem(count):
    return [pl.BlockSpec(memory_space=pltpu.VMEM)] * count


PARAMS = dict(compiler_params=pltpu.CompilerParams(vmem_limit_bytes=32 * 1024 * 1024))


def permute(array, distances):
    shards, helpers = lax.axis_size("shard"), lax.axis_size("rep")
    pairs = [
        (s * helpers + r, (s ^ distances[r]) * helpers + r)
        for s in range(shards)
        for r in range(helpers)
        if distances[r]
    ]
    return lax.ppermute(array, ("shard", "rep"), pairs)


def swap(array, mask):
    return lax.ppermute(array, "rep", [(r, r ^ mask) for r in range(lax.axis_size("rep"))])


def per_device(embeddings, members):
    shards = lax.axis_size("shard")
    helpers = lax.axis_size("rep")
    rows_dev, width = embeddings.shape
    capacity = members.shape[1]
    send_cap = capacity // shards
    stripe = capacity // helpers

    half = send_cap // 2
    reps = range(helpers)
    zero = [0] * helpers
    far = ([shards - 4 + (r >> 1) for r in reps], [half * (r & 1) for r in reps])
    pairs = [([d + (r & 1) for r in reps], zero) for d in (shards - 2, shards - 6)]
    near = ([1] * helpers, zero)
    rounds = [far] + pairs + [near]
    chunks = [(zero, zero), near]
    chunks += pairs + [([d[r ^ 1] for r in reps], zero) for d, _ in pairs]
    chunks += [far, ([far[0][r ^ 2] for r in reps], far[1])]

    wanted = [permute(members, d) for d, _ in rounds]

    def rows(count):
        return jax.ShapeDtypeStruct((count, width), jnp.bfloat16)

    tick = pl.pallas_call(
        zero_kernel,
        out_shape=jax.ShapeDtypeStruct((8, LANES), jnp.float32),
        out_specs=vmem(1)[0],
        cost_estimate=pl.CostEstimate(flops=5 * 10**8, bytes_accessed=2**12, transcendentals=0),
        **PARAMS,
    )()
    sent = []
    after = tick
    for group in ([0], [1], [2, 3]):
        sent += pl.pallas_call(
            functools.partial(select_kernel, [rounds[t] for t in group], send_cap),
            out_shape=tuple(rows(half if t == 0 else send_cap) for t in group),
            in_specs=vmem(len(group) + 2),
            out_specs=tuple(vmem(len(group))),
            cost_estimate=pl.CostEstimate(flops=10**9, bytes_accessed=2**12, transcendentals=0),
            **PARAMS,
        )(*[wanted[t] for t in group], embeddings, after)
        after = sent[-1]
    fetched = [permute(part, d) for part, (d, _) in zip(sent, rounds)]

    def hand_on(part, flops, *others):
        return pl.pallas_call(
            hand_on_kernel,
            out_shape=rows(part.shape[0]),
            in_specs=vmem(1 + len(others)),
            out_specs=vmem(1)[0],
            input_output_aliases={0: 0},
            cost_estimate=pl.CostEstimate(flops=flops, bytes_accessed=2**12, transcendentals=0),
            **PARAMS,
        )(part, *others)

    fetched[0] = hand_on(fetched[0], 300000000)
    place, own = pl.pallas_call(
        functools.partial(place_kernel, chunks, send_cap),
        out_shape=(jax.ShapeDtypeStruct((len(chunks), send_cap), jnp.float32), rows(send_cap)),
        in_specs=vmem(3),
        out_specs=tuple(vmem(2)),
        cost_estimate=pl.CostEstimate(flops=300000000, bytes_accessed=2**12, transcendentals=0),
        **PARAMS,
    )(members, embeddings, fetched[0])
    fetched[2] = hand_on(fetched[2], 10**6, place)
    crossed = hand_on(swap(fetched[0], 2), 1500000000)
    parts = [own] + fetched[1:-1] + [swap(part, 1) for part in fetched[1:-1]]
    parts += [fetched[0], swap(fetched[0], 1), crossed, swap(crossed, 1), fetched[-1]]
    return pl.pallas_call(
        functools.partial(best_kernel, stripe),
        out_shape=jax.ShapeDtypeStruct((1, stripe), jnp.float32),
        in_specs=vmem(len(parts) + 1),
        out_specs=vmem(1)[0],
        scratch_shapes=[pltpu.VMEM((capacity, width), jnp.bfloat16)],
        cost_estimate=pl.CostEstimate(flops=10**9, bytes_accessed=2 * 2**20, transcendentals=0),
        **PARAMS,
    )(place, *parts)


def unit_rows(embeddings):
    values = embeddings.astype(jnp.float32)
    total = jnp.sum(values * values, axis=1, keepdims=True)
    return (values * lax.rsqrt(total + 1e-06)).astype(jnp.bfloat16)


def fetch_rows(unit, wanted):
    picked = jnp.take(unit, jnp.maximum(wanted, 0), axis=0)
    return jnp.where((wanted >= 0)[..., None], picked, jnp.zeros_like(picked))


def running_best(queries, positions, gathered, block_count, key_block):

    def update(block_index, current):
        start = block_index * key_block
        keys = lax.dynamic_slice_in_dim(gathered, start, key_block, 0)
        scores = lax.dot_general(
            queries, keys, (((1,), (1,)), ((), ())), preferred_element_type=jnp.float32
        )
        key_index = start + jnp.arange(key_block, dtype=jnp.int32)
        masked = jnp.where(
            key_index[None, :] < positions[:, None], scores, jnp.full_like(scores, -2.0)
        )
        return jnp.maximum(current, jnp.max(masked, axis=1))

    initial = jnp.full((queries.shape[0],), -1.0, jnp.float32)
    return lax.fori_loop(jnp.int32(0), block_count, update, initial)


def per_device_many(embeddings, members):
    shards = lax.axis_size("shard")
    helpers = lax.axis_size("rep")
    helper_index = lax.axis_index("rep")
    rows_dev = embeddings.shape[0]
    width = embeddings.shape[1]
    capacity = members.shape[1]
    send_cap = capacity // shards
    unit = unit_rows(embeddings)
    row_ids = members[0]
    valid = row_ids >= 0
    count = jnp.sum(valid.astype(jnp.int32))
    source = jnp.where(valid, row_ids // rows_dev, -1)
    local_row = jnp.where(valid, row_ids - source * rows_dev, -1)
    onehot = (source[:, None] == jnp.arange(shards, dtype=jnp.int32)[None, :]).astype(jnp.int32)
    earlier = jnp.cumsum(onehot, axis=0) - onehot
    position = jnp.sum(earlier * onehot, axis=1)
    table_size = shards * send_cap
    flat_index = jnp.where(valid, source * send_cap + position, table_size)
    requests = jnp.full((table_size + 1,), -1, jnp.int32).at[flat_index].set(local_row)
    requests = requests[:table_size].reshape(shards, send_cap)
    wanted = lax.all_to_all(requests, "shard", split_axis=0, concat_axis=0, tiled=True)
    returned = lax.all_to_all(
        fetch_rows(unit, wanted), "shard", split_axis=0, concat_axis=0, tiled=True
    )
    table = returned.reshape(table_size, width)
    picked = jnp.take(table, jnp.minimum(flat_index, table_size - 1), axis=0)
    gathered = jnp.where(valid[:, None], picked, jnp.zeros_like(picked))
    stripe = capacity // helpers
    queries_all = lax.dynamic_slice_in_dim(gathered, helper_index * stripe, stripe, 0)
    positions_all = helper_index * stripe + jnp.arange(stripe, dtype=jnp.int32)
    key_block = min(512, capacity)
    needed = jnp.minimum(count, positions_all[-1])
    block_count = (needed + key_block - 1) // key_block
    values = running_best(queries_all, positions_all, gathered, block_count, key_block)
    pieces = jnp.where(positions_all < count, values, jnp.zeros_like(values))
    return pieces[None, :]


def solution(mesh):
    in_specs = (P("shard", None), P("shard", None))
    out_specs = P("shard", "rep")
    few = mesh.shape["shard"] == 8 and mesh.shape["rep"] == 4
    return jax.shard_map(
        per_device if few else per_device_many,
        mesh=mesh,
        in_specs=in_specs,
        out_specs=out_specs,
        check_vma=False,
    )
```

```python
import functools

import jax
import jax.numpy as jnp
from jax import lax
from jax.experimental import pallas as pl
from jax.experimental.pallas import tpu as pltpu
from jax.sharding import PartitionSpec as P

LANES = 128
FAR = 1e6


def nt_dot(a, b):
    return lax.dot_general(a, b, (((1,), (1,)), ((), ())), preferred_element_type=jnp.float32)


def dot(a, b):
    return jnp.dot(a, b, preferred_element_type=jnp.float32)


def ones_where(mask):
    return jnp.where(mask, 1.0, 0.0).astype(jnp.bfloat16)


def low_onehot(ids):
    return ones_where(lax.broadcasted_iota(jnp.int32, (LANES, ids.shape[1]), 0) == (ids & (LANES - 1)))


def high_marks(ids, first_row, groups):
    high = (ids - first_row) >> 7
    row = lax.broadcasted_iota(jnp.int32, (2 * groups, ids.shape[1]), 0)
    high = jnp.where(high < 0, groups, high)
    return jnp.where(row < groups, jnp.where(high == row, 1.0, 0.0), jnp.where(high < row - groups, 1.0, 0.0))


def slots_of(found, groups):
    row = lax.broadcasted_iota(jnp.int32, (LANES, 2 * LANES), 0)
    col = lax.broadcasted_iota(jnp.int32, (LANES, 2 * LANES), 1)
    counts = dot(found.astype(jnp.bfloat16), ones_where((row < col) | (col >= LANES)))
    slots = counts[:groups, :LANES] + counts[groups:, LANES:]
    return jnp.where(found[:groups] > 0.0, slots, -1.0)


def selector(slots, numbers):
    return jnp.concatenate([ones_where(slots[h : h + 1, :] == numbers) for h in range(slots.shape[0])], axis=1)


def numbers_from(first, wanted, around):
    return ((lax.broadcasted_iota(jnp.int32, (wanted, LANES), 0) + first) & (around - 1)).astype(jnp.float32)


def by_rep(values):
    rep = lax.axis_index("rep")
    chosen = jnp.int32(values[0])
    for r, value in enumerate(values[1:], 1):
        chosen = jnp.where(rep == r, jnp.int32(value), chosen)
    return chosen


def zero_kernel(out_ref):
    out_ref[...] = jnp.zeros(out_ref.shape, out_ref.dtype)


def pick_rows(slots, numbers, rows):
    values = dot(selector(slots, numbers), rows)
    total = jnp.sum(values * values, axis=1, keepdims=True)
    return (values * lax.rsqrt(total + 1e-06)).astype(jnp.bfloat16)


def place_kernel(chunks, send_cap, ids_ref, rows_ref, *refs):
    place_ref, own_ref = refs[-2:]
    groups = rows_ref.shape[0] // LANES
    ids = ids_ref[...]
    low = low_onehot(ids)
    shard = lax.axis_index("shard")
    highs = [high_marks(ids, (shard ^ by_rep(d)) * groups * LANES, groups) for d, _ in chunks]
    here = jnp.concatenate([high[:groups] for high in highs], axis=0)
    count = here.shape[0]
    member = lax.broadcasted_iota(jnp.int32, (1, ids.shape[1]), 1)
    digits = (member >> 5).astype(jnp.float32), (member & 31).astype(jnp.float32)
    marks = [here] + [high[groups:] for high in highs] + [here * digits[0], here * digits[1]]
    found = nt_dot(jnp.concatenate(marks, axis=0).astype(jnp.bfloat16), low)
    slots = slots_of(found[: 2 * count], count)
    position = found[2 * count : 3 * count] * 32.0 + found[3 * count :]
    diagonal = lax.broadcasted_iota(jnp.int32, (send_cap, send_cap), 0) == lax.broadcasted_iota(
        jnp.int32, (send_cap, send_cap), 1
    )
    for c, (_, first) in enumerate(chunks):
        numbers = numbers_from(by_rep(first), send_cap, send_cap)
        spread = jnp.zeros((send_cap, LANES), jnp.float32)
        for h in range(groups):
            g = c * groups + h
            spread += jnp.where(slots[g : g + 1, :] == numbers, position[g : g + 1, :] + 1.0, 0.0)
        column = jnp.sum(spread, axis=1, keepdims=True)
        line = jnp.sum(jnp.where(diagonal, column, 0.0), axis=0, keepdims=True)
        place_ref[c : c + 1, :] = jnp.where(line > 0.0, line - 1.0, FAR)
    own_ref[...] = pick_rows(slots[:groups], numbers_from(0, send_cap, send_cap), rows_ref[...])


def select_kernel(rounds, send_cap, *refs):
    count = len(rounds)
    ids_refs, rows_ref, out_refs = refs[:count], refs[count], refs[-count:]
    rows_dev = rows_ref.shape[0]
    groups = rows_dev // LANES
    first_row = lax.axis_index("shard") * rows_dev
    hits = []
    for ref in ids_refs:
        ids = ref[...]
        hits.append(nt_dot(high_marks(ids, first_row, groups).astype(jnp.bfloat16), low_onehot(ids)))
    hits = [hit[:groups] for hit in hits] + [hit[groups:] for hit in hits]
    slots = slots_of(jnp.concatenate(hits, axis=0), count * groups)
    rows = rows_ref[...]
    for t in range(count):
        ref = out_refs[t]
        numbers = numbers_from(by_rep(rounds[t][1]), ref.shape[0], send_cap)
        ref[...] = pick_rows(slots[t * groups : (t + 1) * groups], numbers, rows)


def hand_on_kernel(rows_ref, *refs):
    refs[-1][:16, :] = rows_ref[:16, :]


def best_kernel(stripe, *refs):
    place_ref, chunk_refs, out_ref, table_ref = refs[0], refs[1:-2], refs[-2], refs[-1]
    send_cap, start, near = place_ref.shape[1], 0, table_ref.shape[0] - place_ref.shape[1]
    for ref in chunk_refs:
        row = start if start < send_cap else start + send_cap if start < near else start - near + send_cap
        table_ref[row : row + ref.shape[0], :] = ref[...]
        start += ref.shape[0]
    place = place_ref[...]
    places = jnp.concatenate([place[c : c + 1, :] for c in range(place.shape[0])], axis=1)
    first = lax.axis_index("rep") * stripe
    query = (lax.broadcasted_iota(jnp.int32, (stripe, 1), 0) + first).astype(jnp.float32)
    table = table_ref[...]
    queries = dot(ones_where(places == query), table).astype(jnp.bfloat16)
    scores = nt_dot(queries, table)
    best = jnp.max(jnp.where(places < query, scores, -2.0), axis=1, keepdims=True)
    count = jnp.sum(jnp.where(places < FAR, 1.0, 0.0), axis=1, keepdims=True)
    best = jnp.where(query < count, jnp.maximum(best, -1.0), 0.0)
    diagonal = lax.broadcasted_iota(jnp.int32, (LANES, LANES), 0) == lax.broadcasted_iota(
        jnp.int32, (LANES, LANES), 1
    )
    for b in range(stripe // LANES):
        part = best[b * LANES : (b + 1) * LANES, :]
        out_ref[:, b * LANES : (b + 1) * LANES] = jnp.sum(jnp.where(diagonal, part, 0.0), axis=0, keepdims=True)


def vmem(count):
    return [pl.BlockSpec(memory_space=pltpu.VMEM)] * count


PARAMS = dict(compiler_params=pltpu.CompilerParams(vmem_limit_bytes=32 * 1024 * 1024))


def permute(array, distances):
    shards, helpers = lax.axis_size("shard"), lax.axis_size("rep")
    pairs = [
        (s * helpers + r, (s ^ distances[r]) * helpers + r)
        for s in range(shards)
        for r in range(helpers)
        if distances[r]
    ]
    return lax.ppermute(array, ("shard", "rep"), pairs)


def swap(array, mask):
    return lax.ppermute(array, "rep", [(r, r ^ mask) for r in range(lax.axis_size("rep"))])


def per_device(embeddings, members):
    shards = lax.axis_size("shard")
    helpers = lax.axis_size("rep")
    rows_dev, width = embeddings.shape
    capacity = members.shape[1]
    send_cap = capacity // shards
    stripe = capacity // helpers

    half = send_cap // 2
    reps = range(helpers)
    zero = [0] * helpers
    far = ([shards - 4 + (r >> 1) for r in reps], [half * (r & 1) for r in reps])
    pairs = [([d + (r & 1) for r in reps], zero) for d in (shards - 2, shards - 6)]
    near = ([1] * helpers, zero)
    rounds = [far] + pairs + [near]
    chunks = [(zero, zero), near]
    chunks += pairs + [([d[r ^ 1] for r in reps], zero) for d, _ in pairs]
    chunks += [far, ([far[0][r ^ 2] for r in reps], far[1])]

    wanted = [permute(members, d) for d, _ in rounds]

    def rows(count):
        return jax.ShapeDtypeStruct((count, width), jnp.bfloat16)

    tick = pl.pallas_call(
        zero_kernel,
        out_shape=jax.ShapeDtypeStruct((8, LANES), jnp.float32),
        out_specs=vmem(1)[0],
        cost_estimate=pl.CostEstimate(flops=5 * 10**8, bytes_accessed=2**12, transcendentals=0),
        **PARAMS,
    )()
    sent = []
    after = tick
    for group in ([0], [1], [2, 3]):
        sent += pl.pallas_call(
            functools.partial(select_kernel, [rounds[t] for t in group], send_cap),
            out_shape=tuple(rows(half if t == 0 else send_cap) for t in group),
            in_specs=vmem(len(group) + 2),
            out_specs=tuple(vmem(len(group))),
            cost_estimate=pl.CostEstimate(flops=10**9, bytes_accessed=2**12, transcendentals=0),
            **PARAMS,
        )(*[wanted[t] for t in group], embeddings, after)
        after = sent[-1]
    fetched = [permute(part, d) for part, (d, _) in zip(sent, rounds)]

    def hand_on(part, flops, *others):
        return pl.pallas_call(
            hand_on_kernel,
            out_shape=rows(part.shape[0]),
            in_specs=vmem(1 + len(others)),
            out_specs=vmem(1)[0],
            input_output_aliases={0: 0},
            cost_estimate=pl.CostEstimate(flops=flops, bytes_accessed=2**12, transcendentals=0),
            **PARAMS,
        )(part, *others)

    fetched[0] = hand_on(fetched[0], 300000000)
    place, own = pl.pallas_call(
        functools.partial(place_kernel, chunks, send_cap),
        out_shape=(jax.ShapeDtypeStruct((len(chunks), send_cap), jnp.float32), rows(send_cap)),
        in_specs=vmem(3),
        out_specs=tuple(vmem(2)),
        cost_estimate=pl.CostEstimate(flops=300000000, bytes_accessed=2**12, transcendentals=0),
        **PARAMS,
    )(members, embeddings, fetched[0])
    fetched[2] = hand_on(fetched[2], 10**6, place)
    crossed = hand_on(swap(fetched[0], 2), 1500000000)
    parts = [own] + fetched[1:-1] + [swap(part, 1) for part in fetched[1:-1]]
    parts += [fetched[0], swap(fetched[0], 1), crossed, swap(crossed, 1), fetched[-1]]
    return pl.pallas_call(
        functools.partial(best_kernel, stripe),
        out_shape=jax.ShapeDtypeStruct((1, stripe), jnp.float32),
        in_specs=vmem(len(parts) + 1),
        out_specs=vmem(1)[0],
        scratch_shapes=[pltpu.VMEM((capacity, width), jnp.bfloat16)],
        cost_estimate=pl.CostEstimate(flops=10**9, bytes_accessed=2 * 2**20, transcendentals=0),
        **PARAMS,
    )(place, *parts)


def unit_rows(embeddings):
    values = embeddings.astype(jnp.float32)
    total = jnp.sum(values * values, axis=1, keepdims=True)
    return (values * lax.rsqrt(total + 1e-06)).astype(jnp.bfloat16)


def fetch_rows(unit, wanted):
    picked = jnp.take(unit, jnp.maximum(wanted, 0), axis=0)
    return jnp.where((wanted >= 0)[..., None], picked, jnp.zeros_like(picked))


def running_best(queries, positions, gathered, block_count, key_block):

    def update(block_index, current):
        start = block_index * key_block
        keys = lax.dynamic_slice_in_dim(gathered, start, key_block, 0)
        scores = lax.dot_general(
            queries, keys, (((1,), (1,)), ((), ())), preferred_element_type=jnp.float32
        )
        key_index = start + jnp.arange(key_block, dtype=jnp.int32)
        masked = jnp.where(
            key_index[None, :] < positions[:, None], scores, jnp.full_like(scores, -2.0)
        )
        return jnp.maximum(current, jnp.max(masked, axis=1))

    initial = jnp.full((queries.shape[0],), -1.0, jnp.float32)
    return lax.fori_loop(jnp.int32(0), block_count, update, initial)


def per_device_many(embeddings, members):
    shards = lax.axis_size("shard")
    helpers = lax.axis_size("rep")
    helper_index = lax.axis_index("rep")
    rows_dev = embeddings.shape[0]
    width = embeddings.shape[1]
    capacity = members.shape[1]
    send_cap = capacity // shards
    unit = unit_rows(embeddings)
    row_ids = members[0]
    valid = row_ids >= 0
    count = jnp.sum(valid.astype(jnp.int32))
    source = jnp.where(valid, row_ids // rows_dev, -1)
    local_row = jnp.where(valid, row_ids - source * rows_dev, -1)
    onehot = (source[:, None] == jnp.arange(shards, dtype=jnp.int32)[None, :]).astype(jnp.int32)
    earlier = jnp.cumsum(onehot, axis=0) - onehot
    position = jnp.sum(earlier * onehot, axis=1)
    table_size = shards * send_cap
    flat_index = jnp.where(valid, source * send_cap + position, table_size)
    requests = jnp.full((table_size + 1,), -1, jnp.int32).at[flat_index].set(local_row)
    requests = requests[:table_size].reshape(shards, send_cap)
    wanted = lax.all_to_all(requests, "shard", split_axis=0, concat_axis=0, tiled=True)
    returned = lax.all_to_all(
        fetch_rows(unit, wanted), "shard", split_axis=0, concat_axis=0, tiled=True
    )
    table = returned.reshape(table_size, width)
    picked = jnp.take(table, jnp.minimum(flat_index, table_size - 1), axis=0)
    gathered = jnp.where(valid[:, None], picked, jnp.zeros_like(picked))
    stripe = capacity // helpers
    queries_all = lax.dynamic_slice_in_dim(gathered, helper_index * stripe, stripe, 0)
    positions_all = helper_index * stripe + jnp.arange(stripe, dtype=jnp.int32)
    key_block = min(512, capacity)
    needed = jnp.minimum(count, positions_all[-1])
    block_count = (needed + key_block - 1) // key_block
    values = running_best(queries_all, positions_all, gathered, block_count, key_block)
    pieces = jnp.where(positions_all < count, values, jnp.zeros_like(values))
    return pieces[None, :]


def solution(mesh):
    in_specs = (P("shard", None), P("shard", None))
    out_specs = P("shard", "rep")
    few = mesh.shape["shard"] == 8 and mesh.shape["rep"] == 4
    return jax.shard_map(
        per_device if few else per_device_many,
        mesh=mesh,
        in_specs=in_specs,
        out_specs=out_specs,
        check_vma=False,
    )
```

```python
import functools

import jax
import jax.numpy as jnp
from jax import lax
from jax.experimental import pallas as pl
from jax.experimental.pallas import tpu as pltpu
from jax.sharding import PartitionSpec as P

LANES = 128
FAR = 1e6


def nt_dot(a, b):
    return lax.dot_general(a, b, (((1,), (1,)), ((), ())), preferred_element_type=jnp.float32)


def dot(a, b):
    return jnp.dot(a, b, preferred_element_type=jnp.float32)


def ones_where(mask):
    return jnp.where(mask, 1.0, 0.0).astype(jnp.bfloat16)


def low_onehot(ids):
    return ones_where(lax.broadcasted_iota(jnp.int32, (LANES, ids.shape[1]), 0) == (ids & (LANES - 1)))


def high_marks(ids, first_row, groups):
    high = (ids - first_row) >> 7
    row = lax.broadcasted_iota(jnp.int32, (2 * groups, ids.shape[1]), 0)
    high = jnp.where(high < 0, groups, high)
    return jnp.where(row < groups, jnp.where(high == row, 1.0, 0.0), jnp.where(high < row - groups, 1.0, 0.0))


def slots_of(found, groups):
    row = lax.broadcasted_iota(jnp.int32, (LANES, 2 * LANES), 0)
    col = lax.broadcasted_iota(jnp.int32, (LANES, 2 * LANES), 1)
    counts = dot(found.astype(jnp.bfloat16), ones_where((row < col) | (col >= LANES)))
    slots = counts[:groups, :LANES] + counts[groups:, LANES:]
    return jnp.where(found[:groups] > 0.0, slots, -1.0)


def selector(slots, numbers):
    return jnp.concatenate([ones_where(slots[h : h + 1, :] == numbers) for h in range(slots.shape[0])], axis=1)


def numbers_from(first, wanted, around):
    return ((lax.broadcasted_iota(jnp.int32, (wanted, LANES), 0) + first) & (around - 1)).astype(jnp.float32)


def by_rep(values):
    rep = lax.axis_index("rep")
    chosen = jnp.int32(values[0])
    for r, value in enumerate(values[1:], 1):
        chosen = jnp.where(rep == r, jnp.int32(value), chosen)
    return chosen


def zero_kernel(out_ref):
    out_ref[...] = jnp.zeros(out_ref.shape, out_ref.dtype)


def scaled(values):
    total = jnp.sum(values * values, axis=1, keepdims=True)
    return (values * lax.rsqrt(total + 1e-06)).astype(jnp.bfloat16)


def pick_rows(slots, numbers, rows):
    return scaled(dot(selector(slots, numbers), rows))


def place_kernel(chunks, send_cap, ids_ref, rows_ref, *refs):
    place_ref, own_ref = refs[-2:]
    groups = rows_ref.shape[0] // LANES
    ids = ids_ref[...]
    low = low_onehot(ids)
    shard = lax.axis_index("shard")
    highs = [high_marks(ids, (shard ^ by_rep(d)) * groups * LANES, groups) for d, _ in chunks]
    here = jnp.concatenate([high[:groups] for high in highs], axis=0)
    count = here.shape[0]
    member = lax.broadcasted_iota(jnp.int32, (1, ids.shape[1]), 1)
    digits = (member >> 5).astype(jnp.float32), (member & 31).astype(jnp.float32)
    marks = [here] + [high[groups:] for high in highs] + [here * digits[0], here * digits[1]]
    found = nt_dot(jnp.concatenate(marks, axis=0).astype(jnp.bfloat16), low)
    slots = slots_of(found[: 2 * count], count)
    position = found[2 * count : 3 * count] * 32.0 + found[3 * count :]
    diagonal = lax.broadcasted_iota(jnp.int32, (send_cap, send_cap), 0) == lax.broadcasted_iota(
        jnp.int32, (send_cap, send_cap), 1
    )
    for c, (_, first) in enumerate(chunks):
        numbers = numbers_from(by_rep(first), send_cap, send_cap)
        spread = jnp.zeros((send_cap, LANES), jnp.float32)
        for h in range(groups):
            g = c * groups + h
            spread += jnp.where(slots[g : g + 1, :] == numbers, position[g : g + 1, :] + 1.0, 0.0)
        column = jnp.sum(spread, axis=1, keepdims=True)
        line = jnp.sum(jnp.where(diagonal, column, 0.0), axis=0, keepdims=True)
        place_ref[c : c + 1, :] = jnp.where(line > 0.0, line - 1.0, FAR)
    own_ref[...] = pick_rows(slots[:groups], numbers_from(0, send_cap, send_cap), rows_ref[...])


def select_kernel(rounds, send_cap, *refs):
    count = len(rounds)
    ids_refs, rows_ref, out_refs = refs[:count], refs[count], refs[-count:]
    rows_dev = rows_ref.shape[0]
    groups = rows_dev // LANES
    first_row = lax.axis_index("shard") * rows_dev
    hits = []
    for ref in ids_refs:
        ids = ref[...]
        hits.append(nt_dot(high_marks(ids, first_row, groups).astype(jnp.bfloat16), low_onehot(ids)))
    hits = [hit[:groups] for hit in hits] + [hit[groups:] for hit in hits]
    slots = slots_of(jnp.concatenate(hits, axis=0), count * groups)
    marks = []
    for t, ref in enumerate(out_refs):
        numbers = numbers_from(by_rep(rounds[t][1]), ref.shape[0], send_cap)
        marks.append(selector(slots[t * groups : (t + 1) * groups], numbers))
    picked = scaled(dot(jnp.concatenate(marks, axis=0), rows_ref[...]))
    start = 0
    for ref in out_refs:
        ref[...] = picked[start : start + ref.shape[0], :]
        start += ref.shape[0]


def hand_on_kernel(rows_ref, *refs):
    refs[-1][:16, :] = rows_ref[:16, :]


def best_kernel(stripe, *refs):
    place_ref, chunk_refs, out_ref, table_ref = refs[0], refs[1:-2], refs[-2], refs[-1]
    send_cap, start, near = place_ref.shape[1], 0, table_ref.shape[0] - place_ref.shape[1]
    for ref in chunk_refs:
        row = start if start < send_cap else start + send_cap if start < near else start - near + send_cap
        table_ref[row : row + ref.shape[0], :] = ref[...]
        start += ref.shape[0]
    place = place_ref[...]
    places = jnp.concatenate([place[c : c + 1, :] for c in range(place.shape[0])], axis=1)
    first = lax.axis_index("rep") * stripe
    query = (lax.broadcasted_iota(jnp.int32, (stripe, 1), 0) + first).astype(jnp.float32)
    table = table_ref[...]
    queries = dot(ones_where(places == query), table).astype(jnp.bfloat16)
    scores = nt_dot(queries, table)
    best = jnp.max(jnp.where(places < query, scores, -2.0), axis=1, keepdims=True)
    count = jnp.sum(jnp.where(places < FAR, 1.0, 0.0), axis=1, keepdims=True)
    best = jnp.where(query < count, jnp.maximum(best, -1.0), 0.0)
    diagonal = lax.broadcasted_iota(jnp.int32, (LANES, LANES), 0) == lax.broadcasted_iota(
        jnp.int32, (LANES, LANES), 1
    )
    for b in range(stripe // LANES):
        part = best[b * LANES : (b + 1) * LANES, :]
        out_ref[:, b * LANES : (b + 1) * LANES] = jnp.sum(jnp.where(diagonal, part, 0.0), axis=0, keepdims=True)


def vmem(count):
    return [pl.BlockSpec(memory_space=pltpu.VMEM)] * count


PARAMS = dict(compiler_params=pltpu.CompilerParams(vmem_limit_bytes=32 * 1024 * 1024))


def permute(array, distances):
    shards, helpers = lax.axis_size("shard"), lax.axis_size("rep")
    pairs = [
        (s * helpers + r, (s ^ distances[r]) * helpers + r)
        for s in range(shards)
        for r in range(helpers)
        if distances[r]
    ]
    return lax.ppermute(array, ("shard", "rep"), pairs)


def swap(array, mask):
    return lax.ppermute(array, "rep", [(r, r ^ mask) for r in range(lax.axis_size("rep"))])


def per_device(embeddings, members):
    shards = lax.axis_size("shard")
    helpers = lax.axis_size("rep")
    rows_dev, width = embeddings.shape
    capacity = members.shape[1]
    send_cap = capacity // shards
    stripe = capacity // helpers

    half = send_cap // 2
    reps = range(helpers)
    zero = [0] * helpers
    far = ([shards - 4 + (r >> 1) for r in reps], [half * (r & 1) for r in reps])
    pairs = [([d + (r & 1) for r in reps], zero) for d in (shards - 2, shards - 6)]
    near = ([1] * helpers, zero)
    rounds = [far] + pairs + [near]
    chunks = [(zero, zero), near]
    chunks += pairs + [([d[r ^ 1] for r in reps], zero) for d, _ in pairs]
    chunks += [far, ([far[0][r ^ 2] for r in reps], far[1])]

    wanted = [permute(members, d) for d, _ in rounds]

    def rows(count):
        return jax.ShapeDtypeStruct((count, width), jnp.bfloat16)

    tick = pl.pallas_call(
        zero_kernel,
        out_shape=jax.ShapeDtypeStruct((8, LANES), jnp.float32),
        out_specs=vmem(1)[0],
        cost_estimate=pl.CostEstimate(flops=5 * 10**8, bytes_accessed=2**12, transcendentals=0),
        **PARAMS,
    )()
    sent = []
    after = tick
    for group in ([0], [1], [2, 3]):
        sent += pl.pallas_call(
            functools.partial(select_kernel, [rounds[t] for t in group], send_cap),
            out_shape=tuple(rows(half if t == 0 else send_cap) for t in group),
            in_specs=vmem(len(group) + 2),
            out_specs=tuple(vmem(len(group))),
            cost_estimate=pl.CostEstimate(flops=10**9, bytes_accessed=2**12, transcendentals=0),
            **PARAMS,
        )(*[wanted[t] for t in group], embeddings, after)
        after = sent[-1]
    fetched = [permute(part, d) for part, (d, _) in zip(sent, rounds)]

    def hand_on(part, flops, *others):
        return pl.pallas_call(
            hand_on_kernel,
            out_shape=rows(part.shape[0]),
            in_specs=vmem(1 + len(others)),
            out_specs=vmem(1)[0],
            input_output_aliases={0: 0},
            cost_estimate=pl.CostEstimate(flops=flops, bytes_accessed=2**12, transcendentals=0),
            **PARAMS,
        )(part, *others)

    fetched[0] = hand_on(fetched[0], 300000000)
    place, own = pl.pallas_call(
        functools.partial(place_kernel, chunks, send_cap),
        out_shape=(jax.ShapeDtypeStruct((len(chunks), send_cap), jnp.float32), rows(send_cap)),
        in_specs=vmem(3),
        out_specs=tuple(vmem(2)),
        cost_estimate=pl.CostEstimate(flops=300000000, bytes_accessed=2**12, transcendentals=0),
        **PARAMS,
    )(members, embeddings, fetched[0])
    fetched[2] = hand_on(fetched[2], 10**6, place)
    crossed = hand_on(swap(fetched[0], 2), 1500000000)
    parts = [own] + fetched[1:-1] + [swap(part, 1) for part in fetched[1:-1]]
    parts += [fetched[0], swap(fetched[0], 1), crossed, swap(crossed, 1), fetched[-1]]
    return pl.pallas_call(
        functools.partial(best_kernel, stripe),
        out_shape=jax.ShapeDtypeStruct((1, stripe), jnp.float32),
        in_specs=vmem(len(parts) + 1),
        out_specs=vmem(1)[0],
        scratch_shapes=[pltpu.VMEM((capacity, width), jnp.bfloat16)],
        cost_estimate=pl.CostEstimate(flops=10**9, bytes_accessed=2 * 2**20, transcendentals=0),
        **PARAMS,
    )(place, *parts)


def unit_rows(embeddings):
    values = embeddings.astype(jnp.float32)
    total = jnp.sum(values * values, axis=1, keepdims=True)
    return (values * lax.rsqrt(total + 1e-06)).astype(jnp.bfloat16)


def fetch_rows(unit, wanted):
    picked = jnp.take(unit, jnp.maximum(wanted, 0), axis=0)
    return jnp.where((wanted >= 0)[..., None], picked, jnp.zeros_like(picked))


def running_best(queries, positions, gathered, block_count, key_block):

    def update(block_index, current):
        start = block_index * key_block
        keys = lax.dynamic_slice_in_dim(gathered, start, key_block, 0)
        scores = lax.dot_general(
            queries, keys, (((1,), (1,)), ((), ())), preferred_element_type=jnp.float32
        )
        key_index = start + jnp.arange(key_block, dtype=jnp.int32)
        masked = jnp.where(
            key_index[None, :] < positions[:, None], scores, jnp.full_like(scores, -2.0)
        )
        return jnp.maximum(current, jnp.max(masked, axis=1))

    initial = jnp.full((queries.shape[0],), -1.0, jnp.float32)
    return lax.fori_loop(jnp.int32(0), block_count, update, initial)


def per_device_many(embeddings, members):
    shards = lax.axis_size("shard")
    helpers = lax.axis_size("rep")
    helper_index = lax.axis_index("rep")
    rows_dev = embeddings.shape[0]
    width = embeddings.shape[1]
    capacity = members.shape[1]
    send_cap = capacity // shards
    unit = unit_rows(embeddings)
    row_ids = members[0]
    valid = row_ids >= 0
    count = jnp.sum(valid.astype(jnp.int32))
    source = jnp.where(valid, row_ids // rows_dev, -1)
    local_row = jnp.where(valid, row_ids - source * rows_dev, -1)
    onehot = (source[:, None] == jnp.arange(shards, dtype=jnp.int32)[None, :]).astype(jnp.int32)
    earlier = jnp.cumsum(onehot, axis=0) - onehot
    position = jnp.sum(earlier * onehot, axis=1)
    table_size = shards * send_cap
    flat_index = jnp.where(valid, source * send_cap + position, table_size)
    requests = jnp.full((table_size + 1,), -1, jnp.int32).at[flat_index].set(local_row)
    requests = requests[:table_size].reshape(shards, send_cap)
    wanted = lax.all_to_all(requests, "shard", split_axis=0, concat_axis=0, tiled=True)
    returned = lax.all_to_all(
        fetch_rows(unit, wanted), "shard", split_axis=0, concat_axis=0, tiled=True
    )
    table = returned.reshape(table_size, width)
    picked = jnp.take(table, jnp.minimum(flat_index, table_size - 1), axis=0)
    gathered = jnp.where(valid[:, None], picked, jnp.zeros_like(picked))
    stripe = capacity // helpers
    queries_all = lax.dynamic_slice_in_dim(gathered, helper_index * stripe, stripe, 0)
    positions_all = helper_index * stripe + jnp.arange(stripe, dtype=jnp.int32)
    key_block = min(512, capacity)
    needed = jnp.minimum(count, positions_all[-1])
    block_count = (needed + key_block - 1) // key_block
    values = running_best(queries_all, positions_all, gathered, block_count, key_block)
    pieces = jnp.where(positions_all < count, values, jnp.zeros_like(values))
    return pieces[None, :]


def solution(mesh):
    in_specs = (P("shard", None), P("shard", None))
    out_specs = P("shard", "rep")
    few = mesh.shape["shard"] == 8 and mesh.shape["rep"] == 4
    return jax.shard_map(
        per_device if few else per_device_many,
        mesh=mesh,
        in_specs=in_specs,
        out_specs=out_specs,
        check_vma=False,
    )
```

```python
import functools

import jax
import jax.numpy as jnp
from jax import lax
from jax.experimental import pallas as pl
from jax.experimental.pallas import tpu as pltpu
from jax.sharding import PartitionSpec as P

LANES = 128
FAR = 1e6


def nt_dot(a, b):
    return lax.dot_general(a, b, (((1,), (1,)), ((), ())), preferred_element_type=jnp.float32)


def dot(a, b):
    return jnp.dot(a, b, preferred_element_type=jnp.float32)


def ones_where(mask):
    return jnp.where(mask, 1.0, 0.0).astype(jnp.bfloat16)


def low_onehot(ids):
    return ones_where(lax.broadcasted_iota(jnp.int32, (LANES, ids.shape[1]), 0) == (ids & (LANES - 1)))


def high_marks(ids, first_row, groups):
    high = (ids - first_row) >> 7
    row = lax.broadcasted_iota(jnp.int32, (2 * groups, ids.shape[1]), 0)
    high = jnp.where(high < 0, groups, high)
    return jnp.where(row < groups, jnp.where(high == row, 1.0, 0.0), jnp.where(high < row - groups, 1.0, 0.0))


def slots_of(found, groups):
    row = lax.broadcasted_iota(jnp.int32, (LANES, LANES), 0)
    col = lax.broadcasted_iota(jnp.int32, (LANES, LANES), 1)
    within = dot(found[:groups].astype(jnp.bfloat16), ones_where(row < col))
    slots = within + jnp.sum(found[groups:], axis=1, keepdims=True)
    return jnp.where(found[:groups] > 0.0, slots, -1.0)


def selector(slots, numbers):
    return jnp.concatenate([ones_where(slots[h : h + 1, :] == numbers) for h in range(slots.shape[0])], axis=1)


def numbers_from(first, wanted, around):
    return ((lax.broadcasted_iota(jnp.int32, (wanted, LANES), 0) + first) & (around - 1)).astype(jnp.float32)


def by_rep(values):
    rep = lax.axis_index("rep")
    chosen = jnp.int32(values[0])
    for r, value in enumerate(values[1:], 1):
        chosen = jnp.where(rep == r, jnp.int32(value), chosen)
    return chosen


def zero_kernel(out_ref):
    out_ref[...] = jnp.zeros(out_ref.shape, out_ref.dtype)


def pick_rows(slots, numbers, rows):
    values = dot(selector(slots, numbers), rows)
    total = jnp.sum(values * values, axis=1, keepdims=True)
    return (values * lax.rsqrt(total + 1e-06)).astype(jnp.bfloat16)


def place_kernel(chunks, send_cap, ids_ref, rows_ref, *refs):
    place_ref, own_ref = refs[-2:]
    groups = rows_ref.shape[0] // LANES
    ids = ids_ref[...]
    low = low_onehot(ids)
    shard = lax.axis_index("shard")
    highs = [high_marks(ids, (shard ^ by_rep(d)) * groups * LANES, groups) for d, _ in chunks]
    here = jnp.concatenate([high[:groups] for high in highs], axis=0)
    count = here.shape[0]
    member = lax.broadcasted_iota(jnp.int32, (1, ids.shape[1]), 1)
    digits = (member >> 5).astype(jnp.float32), (member & 31).astype(jnp.float32)
    marks = [here] + [high[groups:] for high in highs] + [here * digits[0], here * digits[1]]
    found = nt_dot(jnp.concatenate(marks, axis=0).astype(jnp.bfloat16), low)
    slots = slots_of(found[: 2 * count], count)
    position = found[2 * count : 3 * count] * 32.0 + found[3 * count :]
    diagonal = lax.broadcasted_iota(jnp.int32, (send_cap, send_cap), 0) == lax.broadcasted_iota(
        jnp.int32, (send_cap, send_cap), 1
    )
    for c, (_, first) in enumerate(chunks):
        numbers = numbers_from(by_rep(first), send_cap, send_cap)
        spread = jnp.zeros((send_cap, LANES), jnp.float32)
        for h in range(groups):
            g = c * groups + h
            spread += jnp.where(slots[g : g + 1, :] == numbers, position[g : g + 1, :] + 1.0, 0.0)
        column = jnp.sum(spread, axis=1, keepdims=True)
        line = jnp.sum(jnp.where(diagonal, column, 0.0), axis=0, keepdims=True)
        place_ref[c : c + 1, :] = jnp.where(line > 0.0, line - 1.0, FAR)
    own_ref[...] = pick_rows(slots[:groups], numbers_from(0, send_cap, send_cap), rows_ref[...])


def select_kernel(rounds, send_cap, *refs):
    count = len(rounds)
    ids_refs, rows_ref, out_refs = refs[:count], refs[count], refs[-count:]
    rows_dev = rows_ref.shape[0]
    groups = rows_dev // LANES
    first_row = lax.axis_index("shard") * rows_dev
    hits = []
    for ref in ids_refs:
        ids = ref[...]
        hits.append(nt_dot(high_marks(ids, first_row, groups).astype(jnp.bfloat16), low_onehot(ids)))
    hits = [hit[:groups] for hit in hits] + [hit[groups:] for hit in hits]
    slots = slots_of(jnp.concatenate(hits, axis=0), count * groups)
    rows = rows_ref[...]
    for t in range(count):
        ref = out_refs[t]
        numbers = numbers_from(by_rep(rounds[t][1]), ref.shape[0], send_cap)
        ref[...] = pick_rows(slots[t * groups : (t + 1) * groups], numbers, rows)


def hand_on_kernel(rows_ref, *refs):
    refs[-1][:16, :] = rows_ref[:16, :]


def best_kernel(stripe, *refs):
    place_ref, chunk_refs, out_ref, table_ref = refs[0], refs[1:-2], refs[-2], refs[-1]
    send_cap, start, near = place_ref.shape[1], 0, table_ref.shape[0] - place_ref.shape[1]
    for ref in chunk_refs:
        row = start if start < send_cap else start + send_cap if start < near else start - near + send_cap
        table_ref[row : row + ref.shape[0], :] = ref[...]
        start += ref.shape[0]
    place = place_ref[...]
    places = jnp.concatenate([place[c : c + 1, :] for c in range(place.shape[0])], axis=1)
    first = lax.axis_index("rep") * stripe
    query = (lax.broadcasted_iota(jnp.int32, (stripe, 1), 0) + first).astype(jnp.float32)
    table = table_ref[...]
    queries = dot(ones_where(places == query), table).astype(jnp.bfloat16)
    scores = nt_dot(queries, table)
    best = jnp.max(jnp.where(places < query, scores, -2.0), axis=1, keepdims=True)
    count = jnp.sum(jnp.where(places < FAR, 1.0, 0.0), axis=1, keepdims=True)
    best = jnp.where(query < count, jnp.maximum(best, -1.0), 0.0)
    diagonal = lax.broadcasted_iota(jnp.int32, (LANES, LANES), 0) == lax.broadcasted_iota(
        jnp.int32, (LANES, LANES), 1
    )
    for b in range(stripe // LANES):
        part = best[b * LANES : (b + 1) * LANES, :]
        out_ref[:, b * LANES : (b + 1) * LANES] = jnp.sum(jnp.where(diagonal, part, 0.0), axis=0, keepdims=True)


def vmem(count):
    return [pl.BlockSpec(memory_space=pltpu.VMEM)] * count


PARAMS = dict(compiler_params=pltpu.CompilerParams(vmem_limit_bytes=32 * 1024 * 1024))


def permute(array, distances):
    shards, helpers = lax.axis_size("shard"), lax.axis_size("rep")
    pairs = [
        (s * helpers + r, (s ^ distances[r]) * helpers + r)
        for s in range(shards)
        for r in range(helpers)
        if distances[r]
    ]
    return lax.ppermute(array, ("shard", "rep"), pairs)


def swap(array, mask):
    return lax.ppermute(array, "rep", [(r, r ^ mask) for r in range(lax.axis_size("rep"))])


def per_device(embeddings, members):
    shards = lax.axis_size("shard")
    helpers = lax.axis_size("rep")
    rows_dev, width = embeddings.shape
    capacity = members.shape[1]
    send_cap = capacity // shards
    stripe = capacity // helpers

    half = send_cap // 2
    reps = range(helpers)
    zero = [0] * helpers
    far = ([shards - 4 + (r >> 1) for r in reps], [half * (r & 1) for r in reps])
    pairs = [([d + (r & 1) for r in reps], zero) for d in (shards - 2, shards - 6)]
    near = ([1] * helpers, zero)
    rounds = [far] + pairs + [near]
    chunks = [(zero, zero), near]
    chunks += pairs + [([d[r ^ 1] for r in reps], zero) for d, _ in pairs]
    chunks += [far, ([far[0][r ^ 2] for r in reps], far[1])]

    wanted = [permute(members, d) for d, _ in rounds]

    def rows(count):
        return jax.ShapeDtypeStruct((count, width), jnp.bfloat16)

    tick = pl.pallas_call(
        zero_kernel,
        out_shape=jax.ShapeDtypeStruct((8, LANES), jnp.float32),
        out_specs=vmem(1)[0],
        cost_estimate=pl.CostEstimate(flops=5 * 10**8, bytes_accessed=2**12, transcendentals=0),
        **PARAMS,
    )()
    sent = []
    after = tick
    for group in ([0], [1], [2, 3]):
        sent += pl.pallas_call(
            functools.partial(select_kernel, [rounds[t] for t in group], send_cap),
            out_shape=tuple(rows(half if t == 0 else send_cap) for t in group),
            in_specs=vmem(len(group) + 2),
            out_specs=tuple(vmem(len(group))),
            cost_estimate=pl.CostEstimate(flops=10**9, bytes_accessed=2**12, transcendentals=0),
            **PARAMS,
        )(*[wanted[t] for t in group], embeddings, after)
        after = sent[-1]
    fetched = [permute(part, d) for part, (d, _) in zip(sent, rounds)]

    def hand_on(part, flops, *others):
        return pl.pallas_call(
            hand_on_kernel,
            out_shape=rows(part.shape[0]),
            in_specs=vmem(1 + len(others)),
            out_specs=vmem(1)[0],
            input_output_aliases={0: 0},
            cost_estimate=pl.CostEstimate(flops=flops, bytes_accessed=2**12, transcendentals=0),
            **PARAMS,
        )(part, *others)

    fetched[0] = hand_on(fetched[0], 300000000)
    place, own = pl.pallas_call(
        functools.partial(place_kernel, chunks, send_cap),
        out_shape=(jax.ShapeDtypeStruct((len(chunks), send_cap), jnp.float32), rows(send_cap)),
        in_specs=vmem(3),
        out_specs=tuple(vmem(2)),
        cost_estimate=pl.CostEstimate(flops=300000000, bytes_accessed=2**12, transcendentals=0),
        **PARAMS,
    )(members, embeddings, fetched[0])
    fetched[2] = hand_on(fetched[2], 10**6, place)
    crossed = hand_on(swap(fetched[0], 2), 1500000000)
    parts = [own] + fetched[1:-1] + [swap(part, 1) for part in fetched[1:-1]]
    parts += [fetched[0], swap(fetched[0], 1), crossed, swap(crossed, 1), fetched[-1]]
    return pl.pallas_call(
        functools.partial(best_kernel, stripe),
        out_shape=jax.ShapeDtypeStruct((1, stripe), jnp.float32),
        in_specs=vmem(len(parts) + 1),
        out_specs=vmem(1)[0],
        scratch_shapes=[pltpu.VMEM((capacity, width), jnp.bfloat16)],
        cost_estimate=pl.CostEstimate(flops=10**9, bytes_accessed=2 * 2**20, transcendentals=0),
        **PARAMS,
    )(place, *parts)


def unit_rows(embeddings):
    values = embeddings.astype(jnp.float32)
    total = jnp.sum(values * values, axis=1, keepdims=True)
    return (values * lax.rsqrt(total + 1e-06)).astype(jnp.bfloat16)


def fetch_rows(unit, wanted):
    picked = jnp.take(unit, jnp.maximum(wanted, 0), axis=0)
    return jnp.where((wanted >= 0)[..., None], picked, jnp.zeros_like(picked))


def running_best(queries, positions, gathered, block_count, key_block):

    def update(block_index, current):
        start = block_index * key_block
        keys = lax.dynamic_slice_in_dim(gathered, start, key_block, 0)
        scores = lax.dot_general(
            queries, keys, (((1,), (1,)), ((), ())), preferred_element_type=jnp.float32
        )
        key_index = start + jnp.arange(key_block, dtype=jnp.int32)
        masked = jnp.where(
            key_index[None, :] < positions[:, None], scores, jnp.full_like(scores, -2.0)
        )
        return jnp.maximum(current, jnp.max(masked, axis=1))

    initial = jnp.full((queries.shape[0],), -1.0, jnp.float32)
    return lax.fori_loop(jnp.int32(0), block_count, update, initial)


def per_device_many(embeddings, members):
    shards = lax.axis_size("shard")
    helpers = lax.axis_size("rep")
    helper_index = lax.axis_index("rep")
    rows_dev = embeddings.shape[0]
    width = embeddings.shape[1]
    capacity = members.shape[1]
    send_cap = capacity // shards
    unit = unit_rows(embeddings)
    row_ids = members[0]
    valid = row_ids >= 0
    count = jnp.sum(valid.astype(jnp.int32))
    source = jnp.where(valid, row_ids // rows_dev, -1)
    local_row = jnp.where(valid, row_ids - source * rows_dev, -1)
    onehot = (source[:, None] == jnp.arange(shards, dtype=jnp.int32)[None, :]).astype(jnp.int32)
    earlier = jnp.cumsum(onehot, axis=0) - onehot
    position = jnp.sum(earlier * onehot, axis=1)
    table_size = shards * send_cap
    flat_index = jnp.where(valid, source * send_cap + position, table_size)
    requests = jnp.full((table_size + 1,), -1, jnp.int32).at[flat_index].set(local_row)
    requests = requests[:table_size].reshape(shards, send_cap)
    wanted = lax.all_to_all(requests, "shard", split_axis=0, concat_axis=0, tiled=True)
    returned = lax.all_to_all(
        fetch_rows(unit, wanted), "shard", split_axis=0, concat_axis=0, tiled=True
    )
    table = returned.reshape(table_size, width)
    picked = jnp.take(table, jnp.minimum(flat_index, table_size - 1), axis=0)
    gathered = jnp.where(valid[:, None], picked, jnp.zeros_like(picked))
    stripe = capacity // helpers
    queries_all = lax.dynamic_slice_in_dim(gathered, helper_index * stripe, stripe, 0)
    positions_all = helper_index * stripe + jnp.arange(stripe, dtype=jnp.int32)
    key_block = min(512, capacity)
    needed = jnp.minimum(count, positions_all[-1])
    block_count = (needed + key_block - 1) // key_block
    values = running_best(queries_all, positions_all, gathered, block_count, key_block)
    pieces = jnp.where(positions_all < count, values, jnp.zeros_like(values))
    return pieces[None, :]


def solution(mesh):
    in_specs = (P("shard", None), P("shard", None))
    out_specs = P("shard", "rep")
    few = mesh.shape["shard"] == 8 and mesh.shape["rep"] == 4
    return jax.shard_map(
        per_device if few else per_device_many,
        mesh=mesh,
        in_specs=in_specs,
        out_specs=out_specs,
        check_vma=False,
    )
```

```python
import functools

import jax
import jax.numpy as jnp
from jax import lax
from jax.experimental import pallas as pl
from jax.experimental.pallas import tpu as pltpu
from jax.sharding import PartitionSpec as P

LANES = 128
FAR = 1e6


def nt_dot(a, b):
    return lax.dot_general(a, b, (((1,), (1,)), ((), ())), preferred_element_type=jnp.float32)


def dot(a, b):
    return jnp.dot(a, b, preferred_element_type=jnp.float32)


def ones_where(mask):
    return jnp.where(mask, 1.0, 0.0).astype(jnp.bfloat16)


def low_onehot(ids):
    return ones_where(lax.broadcasted_iota(jnp.int32, (LANES, ids.shape[1]), 0) == (ids & (LANES - 1)))


def high_marks(ids, first_row, groups):
    high = (ids - first_row) >> 7
    row = lax.broadcasted_iota(jnp.int32, (2 * groups, ids.shape[1]), 0)
    high = jnp.where(high < 0, groups, high)
    return jnp.where(row < groups, jnp.where(high == row, 1.0, 0.0), jnp.where(high < row - groups, 1.0, 0.0))


def slots_of(found, groups):
    row = lax.broadcasted_iota(jnp.int32, (LANES, 2 * LANES), 0)
    col = lax.broadcasted_iota(jnp.int32, (LANES, 2 * LANES), 1)
    counts = dot(found.astype(jnp.bfloat16), ones_where((row < col) | (col >= LANES)))
    slots = counts[:groups, :LANES] + counts[groups:, LANES:]
    return jnp.where(found[:groups] > 0.0, slots, -1.0)


def selector(slots, numbers):
    return jnp.concatenate([ones_where(slots[h : h + 1, :] == numbers) for h in range(slots.shape[0])], axis=1)


def numbers_from(first, wanted, around):
    return ((lax.broadcasted_iota(jnp.int32, (wanted, LANES), 0) + first) & (around - 1)).astype(jnp.float32)


def by_rep(values):
    rep = lax.axis_index("rep")
    chosen = jnp.int32(values[0])
    for r, value in enumerate(values[1:], 1):
        chosen = jnp.where(rep == r, jnp.int32(value), chosen)
    return chosen


def zero_kernel(out_ref):
    out_ref[...] = jnp.zeros(out_ref.shape, out_ref.dtype)


def pick_rows(slots, numbers, rows):
    values = dot(selector(slots, numbers), rows)
    total = jnp.sum(values * values, axis=1, keepdims=True)
    return (values * lax.rsqrt(total + 1e-06)).astype(jnp.bfloat16)


def place_kernel(chunks, send_cap, ids_ref, rows_ref, *refs):
    place_ref, own_ref = refs[-2:]
    groups = rows_ref.shape[0] // LANES
    ids = ids_ref[...]
    low = low_onehot(ids)
    shard = lax.axis_index("shard")
    highs = [high_marks(ids, (shard ^ by_rep(d)) * groups * LANES, groups) for d, _ in chunks]
    here = jnp.concatenate([high[:groups] for high in highs], axis=0)
    count = here.shape[0]
    member = lax.broadcasted_iota(jnp.int32, (1, ids.shape[1]), 1)
    digits = (member >> 5).astype(jnp.float32), (member & 31).astype(jnp.float32)
    marks = [here] + [high[groups:] for high in highs] + [here * digits[0], here * digits[1]]
    found = nt_dot(jnp.concatenate(marks, axis=0).astype(jnp.bfloat16), low)
    slots = slots_of(found[: 2 * count], count)
    position = found[2 * count : 3 * count] * 32.0 + found[3 * count :]
    diagonal = lax.broadcasted_iota(jnp.int32, (send_cap, send_cap), 0) == lax.broadcasted_iota(
        jnp.int32, (send_cap, send_cap), 1
    )
    for c, (_, first) in enumerate(chunks):
        numbers = numbers_from(by_rep(first), send_cap, send_cap)
        spread = jnp.zeros((send_cap, LANES), jnp.float32)
        for h in range(groups):
            g = c * groups + h
            spread += jnp.where(slots[g : g + 1, :] == numbers, position[g : g + 1, :] + 1.0, 0.0)
        column = jnp.sum(spread, axis=1, keepdims=True)
        line = jnp.sum(jnp.where(diagonal, column, 0.0), axis=0, keepdims=True)
        place_ref[c : c + 1, :] = jnp.where(line > 0.0, line - 1.0, FAR)
    own_ref[...] = pick_rows(slots[:groups], numbers_from(0, send_cap, send_cap), rows_ref[...])


def select_kernel(rounds, send_cap, *refs):
    count = len(rounds)
    ids_refs, rows_ref, out_refs = refs[:count], refs[count], refs[-count:]
    rows_dev = rows_ref.shape[0]
    groups = rows_dev // LANES
    first_row = lax.axis_index("shard") * rows_dev
    hits = []
    for ref in ids_refs:
        ids = ref[...]
        hits.append(nt_dot(high_marks(ids, first_row, groups).astype(jnp.bfloat16), low_onehot(ids)))
    hits = [hit[:groups] for hit in hits] + [hit[groups:] for hit in hits]
    slots = slots_of(jnp.concatenate(hits, axis=0), count * groups)
    rows = rows_ref[...]
    for t in range(count):
        ref = out_refs[t]
        numbers = numbers_from(by_rep(rounds[t][1]), ref.shape[0], send_cap)
        ref[...] = pick_rows(slots[t * groups : (t + 1) * groups], numbers, rows)


def hand_on_kernel(rows_ref, *refs):
    refs[-1][:16, :] = rows_ref[:16, :]


def best_kernel(stripe, *refs):
    place_ref, chunk_refs, out_ref, table_ref = refs[0], refs[1:-2], refs[-2], refs[-1]
    send_cap, start, near = place_ref.shape[1], 0, table_ref.shape[0] - place_ref.shape[1]
    for ref in chunk_refs:
        row = start if start < send_cap else start + send_cap if start < near else start - near + send_cap
        table_ref[row : row + ref.shape[0], :] = ref[...]
        start += ref.shape[0]
    place = place_ref[...]
    places = jnp.concatenate([place[c : c + 1, :] for c in range(place.shape[0])], axis=1)
    first = lax.axis_index("rep") * stripe
    query = (lax.broadcasted_iota(jnp.int32, (stripe, 1), 0) + first).astype(jnp.float32)
    table = table_ref[...]
    queries = dot(ones_where(places == query), table).astype(jnp.bfloat16)
    scores = nt_dot(queries, table)
    best = jnp.max(jnp.where(places < query, scores, -2.0), axis=1, keepdims=True)
    count = jnp.sum(jnp.where(places < FAR, 1.0, 0.0), axis=1, keepdims=True)
    best = jnp.where(query < count, jnp.maximum(best, -1.0), 0.0)
    diagonal = lax.broadcasted_iota(jnp.int32, (LANES, LANES), 0) == lax.broadcasted_iota(
        jnp.int32, (LANES, LANES), 1
    )
    for b in range(stripe // LANES):
        part = best[b * LANES : (b + 1) * LANES, :]
        out_ref[:, b * LANES : (b + 1) * LANES] = jnp.sum(jnp.where(diagonal, part, 0.0), axis=0, keepdims=True)


def vmem(count):
    return [pl.BlockSpec(memory_space=pltpu.VMEM)] * count


PARAMS = dict(compiler_params=pltpu.CompilerParams(vmem_limit_bytes=32 * 1024 * 1024))


def permute(array, distances):
    shards, helpers = lax.axis_size("shard"), lax.axis_size("rep")
    pairs = [
        (s * helpers + r, (s ^ distances[r]) * helpers + r)
        for s in range(shards)
        for r in range(helpers)
        if distances[r]
    ]
    return lax.ppermute(array, ("shard", "rep"), pairs)


def swap(array, mask):
    return lax.ppermute(array, "rep", [(r, r ^ mask) for r in range(lax.axis_size("rep"))])


def per_device(embeddings, members):
    shards = lax.axis_size("shard")
    helpers = lax.axis_size("rep")
    rows_dev, width = embeddings.shape
    capacity = members.shape[1]
    send_cap = capacity // shards
    stripe = capacity // helpers

    half = send_cap // 2
    reps = range(helpers)
    zero = [0] * helpers
    far = ([shards - 4 + (r >> 1) for r in reps], [half * (r & 1) for r in reps])
    pairs = [([shards - 2 + (r & 1) for r in reps], zero), ([shards - 6 + (r & 1 ^ 1 - (r >> 1)) for r in reps], zero)]
    near = ([1] * helpers, zero)
    rounds = [far] + pairs + [near]
    chunks = [(zero, zero), near]
    chunks += pairs + [([d[r ^ 1] for r in reps], zero) for d, _ in pairs]
    chunks += [far, ([far[0][r ^ 2] for r in reps], far[1])]

    wanted = [permute(members, d) for d, _ in rounds]

    def rows(count):
        return jax.ShapeDtypeStruct((count, width), jnp.bfloat16)

    tick = pl.pallas_call(
        zero_kernel,
        out_shape=jax.ShapeDtypeStruct((8, LANES), jnp.float32),
        out_specs=vmem(1)[0],
        cost_estimate=pl.CostEstimate(flops=5 * 10**8, bytes_accessed=2**12, transcendentals=0),
        **PARAMS,
    )()
    sent = []
    after = tick
    for group in ([0], [1], [2, 3]):
        sent += pl.pallas_call(
            functools.partial(select_kernel, [rounds[t] for t in group], send_cap),
            out_shape=tuple(rows(half if t == 0 else send_cap) for t in group),
            in_specs=vmem(len(group) + 2),
            out_specs=tuple(vmem(len(group))),
            cost_estimate=pl.CostEstimate(flops=10**9, bytes_accessed=2**12, transcendentals=0),
            **PARAMS,
        )(*[wanted[t] for t in group], embeddings, after)
        after = sent[-1]
    fetched = [permute(part, d) for part, (d, _) in zip(sent, rounds)]

    def hand_on(part, flops, *others):
        return pl.pallas_call(
            hand_on_kernel,
            out_shape=rows(part.shape[0]),
            in_specs=vmem(1 + len(others)),
            out_specs=vmem(1)[0],
            input_output_aliases={0: 0},
            cost_estimate=pl.CostEstimate(flops=flops, bytes_accessed=2**12, transcendentals=0),
            **PARAMS,
        )(part, *others)

    fetched[0] = hand_on(fetched[0], 300000000)
    place, own = pl.pallas_call(
        functools.partial(place_kernel, chunks, send_cap),
        out_shape=(jax.ShapeDtypeStruct((len(chunks), send_cap), jnp.float32), rows(send_cap)),
        in_specs=vmem(3),
        out_specs=tuple(vmem(2)),
        cost_estimate=pl.CostEstimate(flops=300000000, bytes_accessed=2**12, transcendentals=0),
        **PARAMS,
    )(members, embeddings, fetched[0])
    fetched[2] = hand_on(fetched[2], 10**6, place)
    crossed = hand_on(swap(fetched[0], 2), 1500000000)
    parts = [own] + fetched[1:-1] + [swap(part, 1) for part in fetched[1:-1]]
    parts += [fetched[0], swap(fetched[0], 1), crossed, swap(crossed, 1), fetched[-1]]
    return pl.pallas_call(
        functools.partial(best_kernel, stripe),
        out_shape=jax.ShapeDtypeStruct((1, stripe), jnp.float32),
        in_specs=vmem(len(parts) + 1),
        out_specs=vmem(1)[0],
        scratch_shapes=[pltpu.VMEM((capacity, width), jnp.bfloat16)],
        cost_estimate=pl.CostEstimate(flops=10**9, bytes_accessed=2 * 2**20, transcendentals=0),
        **PARAMS,
    )(place, *parts)


def unit_rows(embeddings):
    values = embeddings.astype(jnp.float32)
    total = jnp.sum(values * values, axis=1, keepdims=True)
    return (values * lax.rsqrt(total + 1e-06)).astype(jnp.bfloat16)


def fetch_rows(unit, wanted):
    picked = jnp.take(unit, jnp.maximum(wanted, 0), axis=0)
    return jnp.where((wanted >= 0)[..., None], picked, jnp.zeros_like(picked))


def running_best(queries, positions, gathered, block_count, key_block):

    def update(block_index, current):
        start = block_index * key_block
        keys = lax.dynamic_slice_in_dim(gathered, start, key_block, 0)
        scores = lax.dot_general(
            queries, keys, (((1,), (1,)), ((), ())), preferred_element_type=jnp.float32
        )
        key_index = start + jnp.arange(key_block, dtype=jnp.int32)
        masked = jnp.where(
            key_index[None, :] < positions[:, None], scores, jnp.full_like(scores, -2.0)
        )
        return jnp.maximum(current, jnp.max(masked, axis=1))

    initial = jnp.full((queries.shape[0],), -1.0, jnp.float32)
    return lax.fori_loop(jnp.int32(0), block_count, update, initial)


def per_device_many(embeddings, members):
    shards = lax.axis_size("shard")
    helpers = lax.axis_size("rep")
    helper_index = lax.axis_index("rep")
    rows_dev = embeddings.shape[0]
    width = embeddings.shape[1]
    capacity = members.shape[1]
    send_cap = capacity // shards
    unit = unit_rows(embeddings)
    row_ids = members[0]
    valid = row_ids >= 0
    count = jnp.sum(valid.astype(jnp.int32))
    source = jnp.where(valid, row_ids // rows_dev, -1)
    local_row = jnp.where(valid, row_ids - source * rows_dev, -1)
    onehot = (source[:, None] == jnp.arange(shards, dtype=jnp.int32)[None, :]).astype(jnp.int32)
    earlier = jnp.cumsum(onehot, axis=0) - onehot
    position = jnp.sum(earlier * onehot, axis=1)
    table_size = shards * send_cap
    flat_index = jnp.where(valid, source * send_cap + position, table_size)
    requests = jnp.full((table_size + 1,), -1, jnp.int32).at[flat_index].set(local_row)
    requests = requests[:table_size].reshape(shards, send_cap)
    wanted = lax.all_to_all(requests, "shard", split_axis=0, concat_axis=0, tiled=True)
    returned = lax.all_to_all(
        fetch_rows(unit, wanted), "shard", split_axis=0, concat_axis=0, tiled=True
    )
    table = returned.reshape(table_size, width)
    picked = jnp.take(table, jnp.minimum(flat_index, table_size - 1), axis=0)
    gathered = jnp.where(valid[:, None], picked, jnp.zeros_like(picked))
    stripe = capacity // helpers
    queries_all = lax.dynamic_slice_in_dim(gathered, helper_index * stripe, stripe, 0)
    positions_all = helper_index * stripe + jnp.arange(stripe, dtype=jnp.int32)
    key_block = min(512, capacity)
    needed = jnp.minimum(count, positions_all[-1])
    block_count = (needed + key_block - 1) // key_block
    values = running_best(queries_all, positions_all, gathered, block_count, key_block)
    pieces = jnp.where(positions_all < count, values, jnp.zeros_like(values))
    return pieces[None, :]


def solution(mesh):
    in_specs = (P("shard", None), P("shard", None))
    out_specs = P("shard", "rep")
    few = mesh.shape["shard"] == 8 and mesh.shape["rep"] == 4
    return jax.shard_map(
        per_device if few else per_device_many,
        mesh=mesh,
        in_specs=in_specs,
        out_specs=out_specs,
        check_vma=False,
    )
```
